1024 devices in a mesh: region: 16 (over z), tile: 64 (over x, y, core).
Axes of the slice: x: 4, y: 8, z: 16, core: 2. Of those that a mesh axis runs over, the one named last changes fastest.
Arguments:
- atm_state: bfloat16 [16384, 1280], P(('region', 'tile')), may hold values from -8 to 8
- ocean_state: float32 [65536, 512], P(('region', 'tile')), may hold values from -6 to 6
- cell_area: float32 [65536, 128], P(('region', 'tile')), may hold values from 1 to 10
- level_weights: float32 [4], replicated, may hold values from 0.1 to 1
- remap: bfloat16 [262144, 32, 128], P(('region', 'tile')), may hold values from 0.0019989014 to 0.059814453
- send_src: int32 [1024, 64, 4], P(('region', 'tile')), may hold values from -1 to 15, as said below
- recv_ocn: int32 [1024, 64, 4], P(('region', 'tile')), may hold values from -1 to 63, as said below
Outputs:
- ocean_flux: float32 [65536, 1024], P(('region', 'tile'))
- atm_flux: float32 [16384, 256], P(('region', 'tile'))
The draws below stay inside these ranges and needn't reach their ends.
Inputs may be any that keep to these rules, and one draw needn't show every extreme that they name: `send_src`: each device fills exactly 128 of its slots; in every region 8 ocean partitions, drawn from the seed, receive all 4 slots from every sender; other entries are -1. `recv_ocn`: an entry is -1 exactly where the matching entry of send_src (sender and receiver exchanged) is -1.
All inputs are finite; a program needn't handle non-finite values.
Results may differ from the reference program's by a relative error of at most 0.0019.
Values may be sent and summed in bfloat16 or wider, within the bound.
A program may use at most 32 MiB of HBM per device.

```python
import math
import jax
import jax.numpy as jnp
from jax import lax

AB = 16
OB = 64
BC = 32
OC = 128
CAP = 4
NF = 10
NLEV = 4
OCH = 4
NFLX = 8
PAIRS = 128
N_POLAR = 8
N_REGION = 16
N_TILE = 64
DEVICES = 1024


def tile_order(region_key):
    return jax.random.permutation(region_key, N_TILE)


def intersection_chosen(key):
    polar_key, score_key = jax.random.split(key)
    ranking = jax.vmap(tile_order)(jax.random.split(polar_key, N_REGION))
    polar = (ranking < N_POLAR).astype(jnp.int32)
    raw_score = jax.random.randint(score_key, (N_REGION, N_TILE, N_TILE, CAP), 0, 1048576)
    score = raw_score + 2097152 * polar[:, None, :, None]
    flat_score = score.reshape(N_REGION, N_TILE, N_TILE * CAP) * (N_TILE * CAP) + jnp.arange(N_TILE * CAP, dtype=jnp.int32)
    order = jnp.argsort(-flat_score, axis=-1)
    ranks = jnp.argsort(order, axis=-1)
    return (ranks < PAIRS).reshape(N_REGION, N_TILE, N_TILE, CAP)


def latitude_band(key):
    band_key = jax.random.fold_in(key, 97)
    return jax.random.uniform(band_key, (N_REGION * N_TILE * OB, 1), jnp.float32)


def draw_send_src(key, part):
    chosen = intersection_chosen(key)
    key = jax.random.fold_in(key, 11)
    source = jax.random.randint(key, (N_REGION, N_TILE, N_TILE, CAP), 0, AB)
    slot_table = jnp.where(chosen, source, -1)
    return slot_table.reshape(N_REGION * N_TILE, N_TILE, CAP).astype(jnp.int32)


def draw_recv_ocn(key, part):
    chosen = intersection_chosen(key)
    key = jax.random.fold_in(key, 23)
    target = jax.random.randint(key, (N_REGION, N_TILE, N_TILE, CAP), 0, OB)
    slot_table = jnp.where(chosen, target, -1).transpose(0, 2, 1, 3)
    return slot_table.reshape(N_REGION * N_TILE, N_TILE, CAP).astype(jnp.int32)


def draw_cell_area(key, part):
    band = latitude_band(key)
    key = jax.random.fold_in(key, 31)
    rough = jax.random.uniform(key, (N_REGION * N_TILE * OB, OC), jnp.float32)
    exponent = 0.7 * band + 0.3 * rough
    return jnp.exp(exponent * math.log(10.0)).astype(jnp.float32)


def draw_ocean_state(key, part):
    band = latitude_band(key)
    key = jax.random.fold_in(key, 47)
    row_count = N_REGION * N_TILE * OB
    noise = jax.random.normal(key, (row_count, OCH * OC), jnp.float32)
    warm = 8.0 * band - 4.0
    offset = jnp.concatenate([jnp.broadcast_to(warm, (row_count, OC)), jnp.zeros((row_count, (OCH - 1) * OC), jnp.float32)], axis=1)
    return jnp.clip(offset + noise, -6.0, 6.0).astype(jnp.float32)


def steps_of(stream_key, shape, shards, smallest, largest):
    def one(axis_at, parts):
        heights = jax.random.uniform(jax.random.fold_in(jax.random.fold_in(stream_key, 6), axis_at), (parts,), jnp.float32, smallest / len(shards), largest / len(shards))
        return jnp.repeat(jnp.exp(heights), shape[axis_at] // parts).reshape((-1,) + (1,) * (len(shape) - axis_at - 1))

    factor_of = one(*shards[0])
    for cut in shards[1:]:
        factor_of = factor_of * one(*cut)
    return factor_of


def gaussian(own_key, dims, spread, limit, shards=(), kind=jnp.bfloat16):
    entries = jax.random.normal(own_key, dims, jnp.float32) * spread
    if len(shards) > 0:
        entries = steps_of(own_key, dims, shards, -0.22, 0.18) * entries
    return jnp.clip(entries, min=-limit, max=limit).astype(kind)


def setup_inputs(seed: int = 0) -> dict:
    streams_of = jax.random.split(jax.random.key(seed), 8)
    atm_state = gaussian(streams_of[0], (DEVICES * AB, NF * NLEV * BC), 2.0, 8.0, ((0, 1024),))
    ocean_state = draw_ocean_state(jax.random.fold_in(streams_of[7], 71), 0)
    cell_area = draw_cell_area(jax.random.fold_in(streams_of[7], 71), 0)
    level_weights = jnp.clip(jnp.exp(jax.random.uniform(streams_of[3], (NLEV,), jnp.float32, math.log(0.1), math.log(1.0))), 0.1, 1.0)
    remap = jnp.clip(jnp.exp(math.log(0.059814453) - 3.3986496 * jax.random.uniform(streams_of[4], (DEVICES * N_TILE * CAP, BC, OC), jnp.float32) ** steps_of(streams_of[4], (DEVICES * N_TILE * CAP, BC, OC), ((0, 1024),), -0.2, 0.2)), 0.0019989014, 0.059814453).astype(jnp.bfloat16)
    send_src = draw_send_src(jax.random.fold_in(streams_of[7], 71), 0)
    recv_ocn = draw_recv_ocn(jax.random.fold_in(streams_of[7], 71), 0)
    return {"atm_state": atm_state, "ocean_state": ocean_state, "cell_area": cell_area, "level_weights": level_weights, "remap": remap, "send_src": send_src, "recv_ocn": recv_ocn}


def bulk_fluxes(remapped, ocean, level_weights):
    block_count = remapped.shape[0]
    cells = remapped.shape[2]
    depth = level_weights.shape[0]
    fields = remapped.reshape(block_count, remapped.shape[1] // depth, depth, cells)
    bottom = jnp.einsum('kflo,l->kfo', fields, level_weights, precision=lax.Precision.HIGHEST)
    surface = ocean.reshape(block_count, 4, cells)
    wind_x = bottom[:, 0] - surface[:, 1]
    wind_y = bottom[:, 1] - surface[:, 2]
    speed = jnp.sqrt(wind_x * wind_x + wind_y * wind_y + bottom[:, 9] * bottom[:, 9] + 1.0)
    transfer = 0.1 * jnp.exp(0.2 * jnp.tanh(bottom[:, 8])) * speed
    stress_x = transfer * wind_x
    stress_y = transfer * wind_y
    sensible = transfer * (bottom[:, 2] - surface[:, 0])
    saturated = jnp.exp(0.1 * surface[:, 0] - 0.1 * jnp.tanh(bottom[:, 7]))
    latent = transfer * (bottom[:, 3] - saturated)
    albedo = 0.05 + 0.3 * jax.nn.sigmoid(surface[:, 3])
    shortwave = (1.0 - albedo) * jax.nn.softplus(bottom[:, 4])
    longwave = jax.nn.softplus(bottom[:, 5]) - 1.0 - 0.2 * surface[:, 0]
    freshwater = jax.nn.softplus(bottom[:, 6]) + latent
    heating = sensible + latent + shortwave + longwave
    return jnp.stack([stress_x, stress_y, sensible, latent, shortwave, longwave, freshwater, heating], axis=1)

def reference(atm_state, ocean_state, cell_area, level_weights, remap, send_src, recv_ocn):
    device_count = N_REGION * N_TILE
    slot_count = N_TILE * CAP
    channels = NF * NLEV

    def receive(device):
        region_base = device // N_TILE * N_TILE
        senders = region_base + jnp.arange(N_TILE, dtype=jnp.int32)
        place = device % N_TILE
        incoming = send_src[senders, place, :]
        row_index = (senders[:, None] * AB + jnp.maximum(incoming, 0)).reshape(slot_count).astype(jnp.int32)
        payload = atm_state[row_index]
        payload = jnp.where((incoming.reshape(slot_count) >= 0)[:, None], payload, jnp.zeros_like(payload))
        weights = lax.dynamic_slice_in_dim(remap, (device * slot_count).astype(jnp.int32), slot_count, 0)
        contrib = jnp.einsum('scb,sbo->sco', payload.reshape(slot_count, channels, BC).astype(jnp.float32), weights.astype(jnp.float32))
        owner = recv_ocn[device].reshape(slot_count)
        selector = (owner[:, None] == jnp.arange(OB, dtype=jnp.int32)[None, :]).astype(jnp.float32)
        remapped = jnp.einsum('sk,sco->kco', selector, contrib, precision=lax.Precision.HIGHEST)
        ocean = lax.dynamic_slice_in_dim(ocean_state, (device * OB).astype(jnp.int32), OB, 0)
        area = lax.dynamic_slice_in_dim(cell_area, (device * OB).astype(jnp.int32), OB, 0)
        raw_flux = bulk_fluxes(remapped, ocean, level_weights)
        return (raw_flux, jnp.sum(area * raw_flux[:, 6, :]), jnp.sum(area))
    raw_all, weighted, areas = lax.map(receive, jnp.arange(device_count, dtype=jnp.int32))
    shift = jnp.sum(weighted) / jnp.sum(areas)
    corrected = raw_all.at[:, :, 6, :].add(-shift)
    ocean_flux = corrected.reshape(device_count * OB, NFLX * OC)

    def send_back(device):
        owner = recv_ocn[device].reshape(slot_count)
        rounded = corrected[device].astype(jnp.bfloat16)
        rows_back = jnp.take(rounded, jnp.maximum(owner, 0), axis=0)
        rows_back = jnp.where((owner >= 0)[:, None, None], rows_back, jnp.zeros_like(rows_back))
        weights = lax.dynamic_slice_in_dim(remap, (device * slot_count).astype(jnp.int32), slot_count, 0)
        back = jnp.einsum('sfo,sbo->sfb', rows_back.astype(jnp.float32), weights.astype(jnp.float32)).astype(jnp.bfloat16)
        return back.reshape(N_TILE, CAP, NFLX * BC)
    backs = lax.map(send_back, jnp.arange(device_count, dtype=jnp.int32))

    def collect(device):
        region_base = device // N_TILE * N_TILE
        place = device % N_TILE
        fetched = backs[region_base + jnp.arange(N_TILE, dtype=jnp.int32), place].reshape(slot_count, NFLX * BC)
        owner = send_src[device].reshape(slot_count)
        selector = (owner[:, None] == jnp.arange(AB, dtype=jnp.int32)[None, :]).astype(jnp.float32)
        return jnp.dot(selector.T, fetched.astype(jnp.float32), precision=lax.Precision.HIGHEST)
    atm_flux = lax.map(collect, jnp.arange(device_count, dtype=jnp.int32)).reshape(device_count * AB, NFLX * BC)
    return (ocean_flux, atm_flux)
```

```python
import functools

import jax
import jax.numpy as jnp
from jax import lax
from jax.experimental import pallas as pl
from jax.experimental.pallas import tpu as pltpu
from jax.sharding import PartitionSpec as P

F32 = jnp.float32
BF16 = jnp.bfloat16
MESH = pl.DeviceIdType.MESH


def iota(shape, axis):
    return lax.broadcasted_iota(jnp.int32, shape, axis)


def two_parts(x):
    high = x.astype(BF16)
    return high, (x - high.astype(F32)).astype(BF16)


def dot(a, b, contract=((1,), (0,))):
    return lax.dot_general(a, b, (contract, ((), ())), preferred_element_type=F32)


def softplus(x):
    return jnp.maximum(x, 0.0) + jnp.log1p(jnp.exp(-jnp.abs(x)))


def fluxes(bottom, surface):
    sst, ocean_u, ocean_v, albedo_in = surface
    wind_x = bottom[0] - ocean_u
    wind_y = bottom[1] - ocean_v
    speed = jnp.sqrt(wind_x * wind_x + wind_y * wind_y + bottom[9] * bottom[9] + 1.0)
    transfer = 0.1 * jnp.exp(0.2 * jnp.tanh(bottom[8])) * speed
    stress_x = transfer * wind_x
    stress_y = transfer * wind_y
    sensible = transfer * (bottom[2] - sst)
    saturated = jnp.exp(0.1 * sst - 0.1 * jnp.tanh(bottom[7]))
    latent = transfer * (bottom[3] - saturated)
    albedo = 0.05 + 0.3 * (1.0 / (1.0 + jnp.exp(-albedo_in)))
    shortwave = (1.0 - albedo) * softplus(bottom[4])
    longwave = softplus(bottom[5]) - 1.0 - 0.2 * sst
    freshwater = softplus(bottom[6]) + latent
    heating = sensible + latent + shortwave + longwave
    return [stress_x, stress_y, sensible, latent, shortwave, longwave, freshwater, heating]


def kernel(
    regions, tiles, atm_ref, ocean_ref, area_ref, weights_ref, remap_ref, src_ref, owner_ref,
    ocean_out, atm_out,
    remap, send1, recv1, contrib, rows_back, send2, recv2, zrows,
    remap_sem, send1_sem, recv1_sem, send2_sem, recv2_sem, zsend_sem, zrecv_sem,
):
    region = lax.axis_index("region")
    tile = lax.axis_index("tile")
    cap = src_ref.shape[1]
    atm_blocks = atm_ref.shape[0]
    ocean_blocks, cells = area_ref.shape
    nf = atm_ref.shape[1] // cells
    columns = cells // cap
    slots = tiles * cap
    nflx = 8
    parts = slots // 8

    load_remap = pltpu.make_async_copy(remap_ref, remap, remap_sem)
    load_remap.start()

    barrier = pltpu.get_barrier_semaphore()

    @pl.loop(1, tiles)
    def _(i):
        peer = lax.rem(tile + i, tiles)
        pl.semaphore_signal(barrier, inc=1, device_id=(region, peer), device_id_type=MESH)

    @pl.loop(1, regions)
    def _(i):
        peer = lax.rem(region + i, regions)
        pl.semaphore_signal(barrier, inc=1, device_id=(peer, tile), device_id_type=MESH)

    lane = iota((atm_blocks, cells), 1)
    level = lane // columns
    level_weight = jnp.zeros((atm_blocks, cells), F32)
    for l in range(cap):
        level_weight = jnp.where(level == l, weights_ref[l], level_weight)
    pieces = []
    for f in range(nf):
        x = atm_ref[:, f * cells : (f + 1) * cells].astype(F32) * level_weight
        x = x + pltpu.roll(x, 2 * columns, 1)
        pieces.append(x + pltpu.roll(x, columns, 1))
    combined = jnp.concatenate(pieces, axis=1)
    block = iota((atm_blocks, nf * cells), 1) % cells // columns
    stacked = jnp.concatenate([jnp.where(block == c, combined, 0.0) for c in range(cap)], axis=0)
    first, rest = two_parts(stacked)
    second = rest
    remainder = stacked - first.astype(F32) - second.astype(F32)
    third = remainder.astype(BF16)
    table = jnp.concatenate([first, second, third], axis=0)
    width = 3 * cap * atm_blocks
    at = iota((width, tiles), 0)
    wanted = jnp.full((width, tiles), -1, jnp.int32)
    for c in range(cap):
        wanted = jnp.where(at // atm_blocks % cap == c, src_ref[0, c : c + 1, :], wanted)
    pick = jnp.where(wanted == at % atm_blocks, 1.0, 0.0).astype(BF16)
    packed = dot(pick, table, ((0,), (0,)))
    for f in range(nf):
        send1[:, f, :] = packed[:, f * cells : (f + 1) * cells]

    repeat = jnp.where(iota((tiles, slots), 1) // cap == iota((tiles, slots), 0), 1.0, 0.0)
    by_slot = dot(owner_ref[0].astype(F32).astype(BF16), repeat.astype(BF16))
    own_row = iota((cap, slots), 0) == iota((cap, slots), 1) % cap
    owner_of = jnp.sum(jnp.where(own_row, by_slot, 0.0), axis=0, keepdims=True)
    feeds = jnp.where(
        owner_of.astype(jnp.int32) == iota((ocean_blocks, slots), 0), 1.0, 0.0
    ).astype(BF16)

    pl.semaphore_wait(barrier, tiles - 1 + regions - 1)

    def exchange(source, target, send_sem, recv_sem):
        @pl.loop(1, tiles)
        def _(i):
            peer = lax.rem(tile + i, tiles)
            pltpu.make_async_remote_copy(
                src_ref=source.at[peer, pl.ds(0, nf)],
                dst_ref=target.at[tile, pl.ds(0, nf)],
                send_sem=send_sem,
                recv_sem=recv_sem,
                device_id=(region, peer),
                device_id_type=MESH,
            ).start()

        target[pl.ds(tile, 1), pl.ds(0, nf), :] = source[pl.ds(tile, 1), pl.ds(0, nf), :]

    def drain(buffer, sem):
        whole = buffer.at[pl.ds(0, tiles - 1), pl.ds(0, nf)]
        pltpu.make_async_copy(whole, whole, sem).wait()

    exchange(send1, recv1, send1_sem, recv1_sem)
    load_remap.wait()
    drain(recv1, recv1_sem)

    row8 = iota((8, cells), 0)
    lane8 = iota((8, cells), 1)
    diagonal = [
        (row8 // cap == h) & (row8 % cap == lane8 // columns) for h in range(8 // cap)
    ]

    @pl.loop(0, parts)
    def _(g):
        halves = []
        for h in range(8 // cap):
            j = g * (8 // cap) + h
            rows = [
                jnp.where(diagonal[h], jnp.broadcast_to(recv1[j, pl.ds(f, 1), :], (8, cells)), 0.0)
                for f in range(nf)
            ]
            halves.append(jnp.concatenate(rows, axis=0))
        high, low = two_parts(jnp.concatenate(halves, axis=1))
        w = remap[pl.ds(pl.multiple_of(g * 8 * columns, 8 * columns), 8 * columns), :]
        out = dot(high, w) + dot(low, w)
        for f in range(nf):
            contrib[pl.ds(pl.multiple_of(g * 8, 8), 8), f * cells : (f + 1) * cells] = out[
                f * 8 : (f + 1) * 8
            ]

    high, low = two_parts(contrib[...])
    bottom = dot(feeds, high) + dot(feeds, low)
    raw = fluxes(
        [bottom[:, f * cells : (f + 1) * cells] for f in range(nf)],
        [ocean_ref[:, f * cells : (f + 1) * cells] for f in range(4)],
    )
    fresh = raw[6]
    for f in range(nflx):
        if f != 6:
            ocean_out[:, f * cells : (f + 1) * cells] = raw[f]

    weighted = jnp.sum(area_ref[...] * fresh, axis=0, keepdims=True)
    total = jnp.sum(area_ref[...], axis=0, keepdims=True)
    half = cells // 2
    low_lanes = iota((1, cells), 1) < half
    sums = jnp.where(
        low_lanes, weighted + pltpu.roll(weighted, half, 1), total + pltpu.roll(total, half, 1)
    )
    zrows[pl.ds(region, 1), pl.ds(0, 1), :] = sums.reshape(1, 1, cells)

    @pl.loop(1, regions)
    def _(i):
        peer = lax.rem(region + i, regions)
        pltpu.make_async_remote_copy(
            src_ref=zrows.at[region, pl.ds(0, 1)],
            dst_ref=zrows.at[region, pl.ds(0, 1)],
            send_sem=zsend_sem,
            recv_sem=zrecv_sem,
            device_id=(peer, tile),
            device_id_type=MESH,
        ).start()

    fresh_high, fresh_low = two_parts(fresh)
    fields = [r.astype(BF16) for r in raw]
    fields[6] = fresh_high
    taken = dot(feeds, jnp.concatenate(fields + [fresh_low], axis=1), ((0,), (0,)))
    rows_back[...] = taken
    ones = jnp.ones((8, cells), F32)

    @pl.loop(0, parts)
    def _(g):
        at_rows = pl.ds(pl.multiple_of(g * 8, 8), 8)
        rows = [rows_back[at_rows, f * cells : (f + 1) * cells] for f in range(nflx + 1)]
        left = jnp.concatenate(rows + [ones], axis=0).astype(BF16)
        w = remap[pl.ds(pl.multiple_of(g * 8 * columns, 8 * columns), 8 * columns), :]
        out = dot(left, w, ((1,), (1,)))
        for h in range(8 // cap):
            j = g * (8 // cap) + h
            piece = out[:, h * cells : (h + 1) * cells]
            for f in range(nflx):
                x = piece[f * 8 : (f + 1) * 8]
                if f == 6:
                    x = x + piece[nflx * 8 : nflx * 8 + 8]
                send2[j, pl.ds(f, 1), :] = jnp.sum(
                    jnp.where(diagonal[h], x, 0.0), axis=0, keepdims=True
                )
            send2[j, pl.ds(nflx, 1), :] = piece[(nflx + 1) * 8 : (nflx + 1) * 8 + 1]

    if regions > 1:
        zs = zrows.at[pl.ds(0, regions - 1), pl.ds(0, 1)]
        pltpu.make_async_copy(zs, zs, zrecv_sem).wait()
    zsum = jnp.sum(zrows[:, 0, :], axis=0, keepdims=True)
    send2[:, nflx + 1, :] = jnp.broadcast_to(zsum, (tiles, cells))

    exchange(send2, recv2, send2_sem, recv2_sem)
    drain(recv2, recv2_sem)

    sums_all = jnp.sum(recv2[:, nflx + 1, :], axis=0, keepdims=True)
    weighted_all = jnp.sum(jnp.where(low_lanes, sums_all, 0.0), axis=1, keepdims=True)
    area_all = jnp.sum(jnp.where(low_lanes, 0.0, sums_all), axis=1, keepdims=True)
    shift = weighted_all / area_all
    ocean_out[:, 6 * cells : 7 * cells] = fresh - shift

    back = []
    for f in range(nflx):
        x = recv2[:, f, :]
        if f == 6:
            x = x - shift * recv2[:, nflx, :]
        back.append(x.astype(BF16))
    gathered = dot(pick[: cap * atm_blocks], jnp.concatenate(back, axis=1))
    group = iota((atm_blocks, cells), 1) // columns
    outs = []
    for f in range(nflx):
        x = jnp.zeros((atm_blocks, cells), F32)
        for c in range(cap):
            x = jnp.where(
                group == c,
                gathered[c * atm_blocks : (c + 1) * atm_blocks, f * cells : (f + 1) * cells],
                x,
            )
        x = x + pltpu.roll(x, 2 * columns, 1)
        outs.append(x + pltpu.roll(x, columns, 1))
    for t in range(nflx // cap):
        x = outs[t * cap]
        for c in range(1, cap):
            x = jnp.where(group == c, outs[t * cap + c], x)
        atm_out[:, t * cells : (t + 1) * cells] = x

    drain(send1, send1_sem)
    drain(send2, send2_sem)
    if regions > 1:
        zs = zrows.at[pl.ds(0, regions - 1), pl.ds(0, 1)]
        pltpu.make_async_copy(zs, zs, zsend_sem).wait()


def per_device(
    regions, tiles, atm_state, ocean_state, cell_area, level_weights, remap, send_src, recv_ocn
):
    cap = send_src.shape[2]
    slots = tiles * cap
    atm_blocks = atm_state.shape[0]
    ocean_blocks, cells = cell_area.shape
    columns = remap.shape[1]
    nf = atm_state.shape[1] // cells
    nflx = 8
    vmem = pl.BlockSpec(memory_space=pltpu.VMEM)
    box = pltpu.VMEM((tiles, 16, cells), F32)
    dma = pltpu.SemaphoreType.DMA
    return pl.pallas_call(
        functools.partial(kernel, regions, tiles),
        out_shape=(
            jax.ShapeDtypeStruct((ocean_blocks, nflx * cells), F32),
            jax.ShapeDtypeStruct((atm_blocks, nflx * columns), F32),
        ),
        in_specs=[
            vmem,
            vmem,
            vmem,
            pl.BlockSpec(memory_space=pltpu.SMEM),
            pl.BlockSpec(memory_space=pl.ANY),
            vmem,
            vmem,
        ],
        out_specs=(vmem, vmem),
        scratch_shapes=[
            pltpu.VMEM((slots * columns, cells), BF16),
            box,
            box,
            pltpu.VMEM((slots, nf * cells), F32),
            pltpu.VMEM((slots, (nflx + 1) * cells), F32),
            box,
            box,
            pltpu.VMEM((regions, 8, cells), F32),
            dma, dma, dma, dma, dma, dma, dma,
        ],
        compiler_params=pltpu.CompilerParams(
            collective_id=0, has_side_effects=True, vmem_limit_bytes=40 * 1024 * 1024
        ),
        cost_estimate=pl.CostEstimate(
            flops=400_000_000, bytes_accessed=4_000_000, transcendentals=100_000
        ),
        name="couple",
    )(
        atm_state, ocean_state, cell_area, level_weights,
        remap.reshape(slots * columns, cells),
        jnp.swapaxes(send_src, 1, 2), jnp.swapaxes(recv_ocn, 1, 2),
    )


def solution(mesh):
    in_specs = (
        P(("region", "tile"), None),
        P(("region", "tile"), None),
        P(("region", "tile"), None),
        P(),
        P(("region", "tile"), None, None),
        P(("region", "tile"), None, None),
        P(("region", "tile"), None, None),
    )
    out_specs = (P(("region", "tile"), None), P(("region", "tile"), None))
    return jax.shard_map(
        functools.partial(per_device, mesh.shape["region"], mesh.shape["tile"]),
        mesh=mesh,
        in_specs=in_specs,
        out_specs=out_specs,
        check_vma=False,
    )
```

```python
import functools

import jax
import jax.numpy as jnp
from jax import lax
from jax.experimental import pallas as pl
from jax.experimental.pallas import tpu as pltpu
from jax.sharding import PartitionSpec as P

F32 = jnp.float32
BF16 = jnp.bfloat16
MESH = pl.DeviceIdType.MESH
CLASSES = 4
FORWARD_UNROLL = 4
BACK_STEP = 4


def iota(shape, axis):
    return lax.broadcasted_iota(jnp.int32, shape, axis)


def two_parts(x):
    high = x.astype(BF16)
    return high, (x - high.astype(F32)).astype(BF16)


def dot(a, b, contract=((1,), (0,))):
    return lax.dot_general(a, b, (contract, ((), ())), preferred_element_type=F32)


def softplus(x):
    return jnp.maximum(x, 0.0) + jnp.log1p(jnp.exp(-jnp.abs(x)))


def fluxes(bottom, surface):
    sst, ocean_u, ocean_v, albedo_in = surface
    wind_x = bottom[0] - ocean_u
    wind_y = bottom[1] - ocean_v
    speed = jnp.sqrt(wind_x * wind_x + wind_y * wind_y + bottom[9] * bottom[9] + 1.0)
    transfer = 0.1 * jnp.exp(0.2 * jnp.tanh(bottom[8])) * speed
    stress_x = transfer * wind_x
    stress_y = transfer * wind_y
    sensible = transfer * (bottom[2] - sst)
    saturated = jnp.exp(0.1 * sst - 0.1 * jnp.tanh(bottom[7]))
    latent = transfer * (bottom[3] - saturated)
    albedo = 0.05 + 0.3 * (1.0 / (1.0 + jnp.exp(-albedo_in)))
    shortwave = (1.0 - albedo) * softplus(bottom[4])
    longwave = softplus(bottom[5]) - 1.0 - 0.2 * sst
    freshwater = softplus(bottom[6]) + latent
    heating = sensible + latent + shortwave + longwave
    return [stress_x, stress_y, sensible, latent, shortwave, longwave, freshwater, heating]


def chip_grid(tiles):
    chips = tiles // 2
    height = min(8, chips)
    return chips // height, height


def outward(k, size):
    step = (k + 1) // 2
    return size // 2 + step * (1 - 2 * (k % 2))


def kernel(
    regions, tiles, atm_hbm, ocean_hbm, area_hbm, weights_ref, remap_hbm, src_hbm, owner_hbm,
    ocean_out, atm_out,
    atm_ref, ocean_ref, area_ref, src_ref, owner_ref,
    remap, send1, recv1, contrib, rows_back, send2, recv2, trows, zrows,
    load_sem, send1_sem, recv1_sem, send2_sem, recv2_sem, tsend_sem, trecv_sem, zsend_sem, zrecv_sem,
):
    region = lax.axis_index("region")
    tile = lax.axis_index("tile")
    cap = src_ref.shape[1]
    atm_blocks = atm_ref.shape[0]
    ocean_blocks, cells = area_ref.shape
    nf = atm_ref.shape[1] // cells
    columns = cells // cap
    slots = tiles * cap
    nflx = 8
    wide, high_grid = chip_grid(tiles)
    chips = tiles // 2
    per_class = chips // CLASSES
    depth = 8 * columns

    loads = [
        pltpu.make_async_copy(source, target, load_sem.at[n])
        for n, (source, target) in enumerate(
            [
                (atm_hbm, atm_ref),
                (src_hbm, src_ref),
                (owner_hbm, owner_ref),
                (ocean_hbm, ocean_ref),
                (area_hbm, area_ref),
                (remap_hbm, remap),
            ]
        )
    ]

    barrier = pltpu.get_barrier_semaphore()
    my_chip = tile // 2
    core = tile % 2

    def chip_at(k, sign):
        away_y = outward(k // wide, high_grid)
        away_x = outward(k % wide, wide)
        x = (my_chip // high_grid + sign * away_x + wide) % wide
        y = (my_chip % high_grid + sign * away_y + high_grid) % high_grid
        return x * high_grid + y

    def peers(visit):
        for n in range(CLASSES):

            @pl.loop(n * per_class, min((n + 1) * per_class, chips - 1))
            def _(k):
                chip = chip_at(k, 1)
                visit(n, chip * 2 + core)
                visit(n, chip * 2 + 1 - core)

        visit(CLASSES - 1, my_chip * 2 + 1 - core)

    @pl.loop(1, regions)
    def _(i):
        peer = (region + i) % regions
        pl.semaphore_signal(barrier, inc=1, device_id=(peer, tile), device_id_type=MESH)

    def greet(_, peer):
        pl.semaphore_signal(barrier, inc=1, device_id=(region, peer), device_id_type=MESH)

    peers(greet)
    for load in loads:
        load.start()
    for load in loads[:3]:
        load.wait()

    lane = iota((atm_blocks, cells), 1)
    level = lane // columns
    level_weight = jnp.zeros((atm_blocks, cells), F32)
    for l in range(cap):
        level_weight = jnp.where(level == l, weights_ref[l], level_weight)
    pieces = []
    for f in range(nf):
        x = atm_ref[:, f * cells : (f + 1) * cells].astype(F32) * level_weight
        x = x + pltpu.roll(x, 2 * columns, 1)
        pieces.append(x + pltpu.roll(x, columns, 1))
    combined = jnp.concatenate(pieces, axis=1)
    block = iota((atm_blocks, nf * cells), 1) % cells // columns
    stacked = jnp.concatenate([jnp.where(block == c, combined, 0.0) for c in range(cap)], axis=0)
    first, second = two_parts(stacked)
    third = (stacked - first.astype(F32) - second.astype(F32)).astype(BF16)
    table = jnp.concatenate([first, second, third], axis=0)
    width = 3 * cap * atm_blocks
    at = iota((width, tiles), 0)
    wanted = jnp.full((width, tiles), -1, jnp.int32)
    for c in range(cap):
        wanted = jnp.where(at // atm_blocks % cap == c, src_ref[0, c : c + 1, :], wanted)
    pick = jnp.where(wanted == at % atm_blocks, 1.0, 0.0).astype(BF16)
    packed = dot(pick, table, ((0,), (0,)))
    for f in range(nf):
        send1[:, f, :] = packed[:, f * cells : (f + 1) * cells]

    at = iota((tiles, slots), 1)
    repeat = jnp.where(at // 8 * 2 + at % 2 == iota((tiles, slots), 0), 1.0, 0.0)
    by_slot = dot(owner_ref[0].astype(F32).astype(BF16), repeat.astype(BF16))
    own_row = iota((cap, slots), 0) == iota((cap, slots), 1) % 8 // 2
    owner_of = jnp.sum(jnp.where(own_row, by_slot, 0.0), axis=0, keepdims=True)
    feeds = jnp.where(
        owner_of.astype(jnp.int32) == iota((ocean_blocks, slots), 0), 1.0, 0.0
    ).astype(BF16)

    recv1[pl.ds(tile, 1), pl.ds(0, nf), :] = send1[pl.ds(tile, 1), pl.ds(0, nf), :]

    pl.semaphore_wait(barrier, tiles - 1 + regions - 1)

    def send(source, target, rows, send_sem, recv_sem, peer):
        pltpu.make_async_remote_copy(
            src_ref=source.at[peer, pl.ds(0, rows)],
            dst_ref=target.at[tile, pl.ds(0, rows)],
            send_sem=send_sem,
            recv_sem=recv_sem,
            device_id=(region, peer),
            device_id_type=MESH,
        ).start()

    def drain(buffer, count, rows, sem):
        whole = buffer.at[pl.ds(0, count), pl.ds(0, rows)]
        pltpu.make_async_copy(whole, whole, sem).wait()

    peers(lambda n, peer: send(send1, recv1, nf, send1_sem, recv1_sem.at[n], peer))

    for load in loads[3:]:
        load.wait()

    row8 = iota((8, cells), 0)
    lane8 = iota((8, cells), 1)
    own_lanes = row8 // 2 == lane8 // columns
    even = row8 % 2 == 0
    diagonal = [own_lanes & even, own_lanes & (row8 % 2 == 1)]

    def group(g):
        return remap[pl.ds(pl.multiple_of(g * depth, depth), depth), :]

    def forward(k):
        g = chip_at(k, -1)
        halves = []
        for h in range(2):
            rows = [
                jnp.where(
                    diagonal[h],
                    jnp.broadcast_to(recv1[g * 2 + h, pl.ds(f, 1), :], (8, cells)),
                    0.0,
                )
                for f in range(nf)
            ]
            halves.append(jnp.concatenate(rows, axis=0))
        high, low = two_parts(jnp.concatenate(halves, axis=1))
        w = group(g)
        out = dot(high, w) + dot(low, w)
        for f in range(nf):
            contrib[pl.ds(pl.multiple_of(g * 8, 8), 8), f * cells : (f + 1) * cells] = out[
                f * 8 : (f + 1) * 8
            ]

    for n in range(CLASSES):
        arriving = 2 * per_class - (n == CLASSES - 1)
        drain(recv1, arriving, nf, recv1_sem.at[n])

        @pl.loop(n * per_class, (n + 1) * per_class, unroll=min(FORWARD_UNROLL, per_class))
        def _(k):
            forward(k)

    high, low = two_parts(contrib[...])
    bottom = dot(feeds, high) + dot(feeds, low)
    raw = fluxes(
        [bottom[:, f * cells : (f + 1) * cells] for f in range(nf)],
        [ocean_ref[:, f * cells : (f + 1) * cells] for f in range(4)],
    )
    fresh = raw[6]

    weighted = jnp.sum(area_ref[...] * fresh, axis=0, keepdims=True)
    total = jnp.sum(area_ref[...], axis=0, keepdims=True)
    half = cells // 2
    low_lanes = iota((1, cells), 1) < half
    sums = jnp.where(
        low_lanes, weighted + pltpu.roll(weighted, half, 1), total + pltpu.roll(total, half, 1)
    )
    trows[pl.ds(tile, 1), pl.ds(0, 1), :] = sums.reshape(1, 1, cells)

    def send_sums(_, peer):
        pltpu.make_async_remote_copy(
            src_ref=trows.at[tile, pl.ds(0, 1)],
            dst_ref=trows.at[tile, pl.ds(0, 1)],
            send_sem=tsend_sem,
            recv_sem=trecv_sem,
            device_id=(region, peer),
            device_id_type=MESH,
        ).start()

    peers(send_sums)

    for f in range(nflx):
        if f != 6:
            ocean_out[:, f * cells : (f + 1) * cells] = raw[f]
    fresh_high, fresh_low = two_parts(fresh)
    fields = [r.astype(BF16) for r in raw]
    fields[6] = fresh_high
    rows_back[...] = dot(feeds, jnp.concatenate(fields + [fresh_low], axis=1), ((0,), (0,)))
    ones = jnp.ones((8, cells), F32)

    def pair(a, b):
        upper = row8 < 4
        return jnp.where(upper, a, b) + pltpu.roll(jnp.where(upper, b, a), 4, 0)

    def four(a, b):
        near = row8 % 4 < 2
        x = jnp.where(near, b, a)
        return jnp.where(near, a, b) + jnp.where(near, pltpu.roll(x, 6, 0), pltpu.roll(x, 2, 0))

    def backward(g):
        at_rows = pl.ds(pl.multiple_of(g * 8, 8), 8)
        rows = [rows_back[at_rows, f * cells : (f + 1) * cells] for f in range(nflx + 1)]
        left = jnp.concatenate(rows + [ones], axis=0).astype(BF16)
        out = dot(left, group(g), ((1,), (1,)))
        x = []
        for f in range(nflx + 1):
            piece = out[f * 8 : (f + 1) * 8]
            mixed = jnp.where(even, piece[:, :cells], piece[:, cells:])
            x.append(jnp.where(own_lanes, mixed, 0.0))
        x[6] = x[6] + x[nflx]
        q0 = four(pair(x[0], x[4]), pair(x[2], x[6]))
        q1 = four(pair(x[1], x[5]), pair(x[3], x[7]))
        send2[g * 2, pl.ds(0, 8), :] = jnp.where(even, q0, pltpu.roll(q1, 1, 0))
        send2[g * 2 + 1, pl.ds(0, 8), :] = jnp.where(even, pltpu.roll(q0, 7, 0), q1)
        for h in range(2):
            at = (nflx + 1) * 8
            send2[g * 2 + h, pl.ds(nflx, 1), :] = out[at : at + 1, h * cells : (h + 1) * cells]

    @pl.loop(0, (chips - 1) // BACK_STEP)
    def _(i):
        for u in range(BACK_STEP):
            backward(chip_at(i * BACK_STEP + u, 1))
        for u in range(BACK_STEP):
            chip = chip_at(i * BACK_STEP + u, 1)
            for peer in (chip * 2 + core, chip * 2 + 1 - core):
                send(send2, recv2, nflx + 1, send2_sem, recv2_sem, peer)

    for k in range((chips - 1) // BACK_STEP * BACK_STEP, chips - 1):
        backward(chip_at(k, 1))
        for peer in (chip_at(k, 1) * 2 + core, chip_at(k, 1) * 2 + 1 - core):
            send(send2, recv2, nflx + 1, send2_sem, recv2_sem, peer)
    backward(my_chip)
    send(send2, recv2, nflx + 1, send2_sem, recv2_sem, my_chip * 2 + 1 - core)
    recv2[pl.ds(tile, 1), pl.ds(0, nflx + 1), :] = send2[pl.ds(tile, 1), pl.ds(0, nflx + 1), :]

    drain(trows, tiles - 1, 1, trecv_sem)
    sums = jnp.sum(trows[:, 0, :], axis=0, keepdims=True)
    zrows[pl.ds(region, 1), pl.ds(0, 1), :] = sums.reshape(1, 1, cells)

    @pl.loop(1, regions)
    def _(i):
        peer = (region + i) % regions
        pltpu.make_async_remote_copy(
            src_ref=zrows.at[region, pl.ds(0, 1)],
            dst_ref=zrows.at[region, pl.ds(0, 1)],
            send_sem=zsend_sem,
            recv_sem=zrecv_sem,
            device_id=(peer, tile),
            device_id_type=MESH,
        ).start()

    drain(recv2, tiles - 1, nflx + 1, recv2_sem)
    if regions > 1:
        drain(zrows, regions - 1, 1, zrecv_sem)
    sums_all = jnp.sum(zrows[:, 0, :], axis=0, keepdims=True)
    weighted_all = jnp.sum(jnp.where(low_lanes, sums_all, 0.0), axis=1, keepdims=True)
    area_all = jnp.sum(jnp.where(low_lanes, 0.0, sums_all), axis=1, keepdims=True)
    shift = weighted_all / area_all
    ocean_out[:, 6 * cells : 7 * cells] = fresh - shift

    back = []
    for f in range(nflx):
        x = recv2[:, f, :]
        if f == 6:
            x = x - shift * recv2[:, nflx, :]
        back.append(x.astype(BF16))
    gathered = dot(pick[: cap * atm_blocks], jnp.concatenate(back, axis=1))
    lane_group = iota((atm_blocks, cells), 1) // columns
    outs = []
    for f in range(nflx):
        x = jnp.zeros((atm_blocks, cells), F32)
        for c in range(cap):
            x = jnp.where(
                lane_group == c,
                gathered[c * atm_blocks : (c + 1) * atm_blocks, f * cells : (f + 1) * cells],
                x,
            )
        x = x + pltpu.roll(x, 2 * columns, 1)
        outs.append(x + pltpu.roll(x, columns, 1))
    for t in range(nflx // cap):
        x = outs[t * cap]
        for c in range(1, cap):
            x = jnp.where(lane_group == c, outs[t * cap + c], x)
        atm_out[:, t * cells : (t + 1) * cells] = x

    drain(send1, tiles - 1, nf, send1_sem)
    drain(send2, tiles - 1, nflx + 1, send2_sem)
    drain(trows, tiles - 1, 1, tsend_sem)
    if regions > 1:
        drain(zrows, regions - 1, 1, zsend_sem)


def per_device(
    regions, tiles, atm_state, ocean_state, cell_area, level_weights, remap, send_src, recv_ocn
):
    cap = send_src.shape[2]
    slots = tiles * cap
    atm_blocks = atm_state.shape[0]
    ocean_blocks, cells = cell_area.shape
    columns = remap.shape[1]
    nf = atm_state.shape[1] // cells
    nflx = 8
    vmem = pl.BlockSpec(memory_space=pltpu.VMEM)
    hbm = pl.BlockSpec(memory_space=pltpu.HBM)
    box = pltpu.VMEM((tiles, 16, cells), F32)
    dma = pltpu.SemaphoreType.DMA
    return pl.pallas_call(
        functools.partial(kernel, regions, tiles),
        out_shape=(
            jax.ShapeDtypeStruct((ocean_blocks, nflx * cells), F32),
            jax.ShapeDtypeStruct((atm_blocks, nflx * columns), F32),
        ),
        in_specs=[hbm, hbm, hbm, pl.BlockSpec(memory_space=pltpu.SMEM), hbm, hbm, hbm],
        out_specs=(vmem, vmem),
        scratch_shapes=[
            pltpu.VMEM(atm_state.shape, BF16),
            pltpu.VMEM(ocean_state.shape, F32),
            pltpu.VMEM(cell_area.shape, F32),
            pltpu.VMEM((1, cap, tiles), jnp.int32),
            pltpu.VMEM((1, cap, tiles), jnp.int32),
            pltpu.VMEM((slots * columns, cells), BF16),
            box,
            box,
            pltpu.VMEM((slots, nf * cells), F32),
            pltpu.VMEM((slots, (nflx + 1) * cells), F32),
            box,
            box,
            pltpu.VMEM((tiles, 8, cells), F32),
            pltpu.VMEM((regions, 8, cells), F32),
            pltpu.SemaphoreType.DMA((6,)),
            dma,
            pltpu.SemaphoreType.DMA((CLASSES,)),
            dma, dma, dma, dma, dma, dma,
        ],
        compiler_params=pltpu.CompilerParams(
            collective_id=0, has_side_effects=True, vmem_limit_bytes=60 * 1024 * 1024
        ),
        cost_estimate=pl.CostEstimate(
            flops=400_000_000, bytes_accessed=4_000_000, transcendentals=100_000
        ),
        name="couple",
    )(
        atm_state, ocean_state, cell_area, level_weights,
        remap.reshape(slots * columns, cells),
        jnp.swapaxes(send_src, 1, 2), jnp.swapaxes(recv_ocn, 1, 2),
    )


def solution(mesh):
    in_specs = (
        P(("region", "tile"), None),
        P(("region", "tile"), None),
        P(("region", "tile"), None),
        P(),
        P(("region", "tile"), None, None),
        P(("region", "tile"), None, None),
        P(("region", "tile"), None, None),
    )
    out_specs = (P(("region", "tile"), None), P(("region", "tile"), None))
    return jax.shard_map(
        functools.partial(per_device, mesh.shape["region"], mesh.shape["tile"]),
        mesh=mesh,
        in_specs=in_specs,
        out_specs=out_specs,
        check_vma=False,
    )
```

```python
import functools

import jax
import jax.numpy as jnp
from jax import lax
from jax.experimental import pallas as pl
from jax.experimental.pallas import tpu as pltpu
from jax.sharding import PartitionSpec as P

F32 = jnp.float32
BF16 = jnp.bfloat16
MESH = pl.DeviceIdType.MESH
CLASSES = 4
FORWARD_UNROLL = 4
BACK_STEP = 4
ROOTS = 2
EARLY = (0, 1, 3, 6, 7, 8, 9)
LATE = (2, 4, 5)
LATE_ROW = 8


def iota(shape, axis):
    return lax.broadcasted_iota(jnp.int32, shape, axis)


def two_parts(x):
    high = x.astype(BF16)
    return high, (x - high.astype(F32)).astype(BF16)


def dot(a, b, contract=((1,), (0,))):
    return lax.dot_general(a, b, (contract, ((), ())), preferred_element_type=F32)


def softplus(x):
    return jnp.maximum(x, 0.0) + jnp.log1p(jnp.exp(-jnp.abs(x)))


def freshwater_flux(bottom, surface):
    sst, ocean_u, ocean_v, _ = surface
    wind_x = bottom[0] - ocean_u
    wind_y = bottom[1] - ocean_v
    speed = jnp.sqrt(wind_x * wind_x + wind_y * wind_y + bottom[9] * bottom[9] + 1.0)
    transfer = 0.1 * jnp.exp(0.2 * jnp.tanh(bottom[8])) * speed
    saturated = jnp.exp(0.1 * sst - 0.1 * jnp.tanh(bottom[7]))
    latent = transfer * (bottom[3] - saturated)
    return transfer, latent, softplus(bottom[6]) + latent


def fluxes(bottom, surface, transfer, latent, freshwater):
    sst, ocean_u, ocean_v, albedo_in = surface
    stress_x = transfer * (bottom[0] - ocean_u)
    stress_y = transfer * (bottom[1] - ocean_v)
    sensible = transfer * (bottom[2] - sst)
    albedo = 0.05 + 0.3 * (1.0 / (1.0 + jnp.exp(-albedo_in)))
    shortwave = (1.0 - albedo) * softplus(bottom[4])
    longwave = softplus(bottom[5]) - 1.0 - 0.2 * sst
    heating = sensible + latent + shortwave + longwave
    return [stress_x, stress_y, sensible, latent, shortwave, longwave, freshwater, heating]


def chip_grid(tiles):
    chips = tiles // 2
    height = min(8, chips)
    return chips // height, height


def outward(k, size):
    step = (k + 1) // 2
    return size // 2 + step * (1 - 2 * (k % 2))


def kernel(
    regions, tiles, atm_hbm, ocean_hbm, area_hbm, weights_ref, remap_hbm, src_hbm, owner_hbm,
    ocean_hbm_out, atm_hbm_out,
    atm_ref, ocean_ref, area_ref, src_ref, owner_ref, ocean_out, atm_out,
    remap, send1, recv1, contrib, total_ref, rows_back, send2, recv2, trows, zrows, zmean,
    load_sem, send1_sem, recv1_sem, send2_sem, recv2_sem, tsend_sem, trecv_sem, zsend_sem, zrecv_sem,
    msend_sem, mrecv_sem, late_send_sem, late_recv_sem, out_sem,
):
    region = lax.axis_index("region")
    tile = lax.axis_index("tile")
    cap = src_ref.shape[1]
    atm_blocks = atm_ref.shape[0]
    ocean_blocks, cells = area_ref.shape
    nf = atm_ref.shape[1] // cells
    columns = cells // cap
    slots = tiles * cap
    nflx = 8
    wide, high_grid = chip_grid(tiles)
    chips = tiles // 2
    per_class = chips // CLASSES
    depth = 8 * columns

    loads = [
        pltpu.make_async_copy(source, target, load_sem.at[n])
        for n, (source, target) in enumerate(
            [
                (atm_hbm, atm_ref),
                (src_hbm, src_ref),
                (owner_hbm, owner_ref),
                (ocean_hbm, ocean_ref),
                (area_hbm, area_ref),
                (remap_hbm, remap),
            ]
        )
    ]

    barrier = pltpu.get_barrier_semaphore()
    my_chip = tile // 2
    core = tile % 2

    def chip_at(k, sign):
        away_y = outward(k // wide, high_grid)
        away_x = outward(k % wide, wide)
        x = (my_chip // high_grid + sign * away_x + wide) % wide
        y = (my_chip % high_grid + sign * away_y + high_grid) % high_grid
        return x * high_grid + y

    def peers(visit):
        for n in range(CLASSES):

            @pl.loop(n * per_class, min((n + 1) * per_class, chips - 1))
            def _(k):
                chip = chip_at(k, 1)
                visit(n, chip * 2 + core)
                visit(n, chip * 2 + 1 - core)

        visit(CLASSES - 1, my_chip * 2 + 1 - core)

    roots = min(ROOTS, regions)
    near, stride = max(regions // 2, roots), regions // 4
    is_root = region < roots
    hands_on = (region >= near - stride) & (region < regions - stride) & (near < regions)
    greeted = jnp.where(is_root, regions - 1, 1)
    reached = jnp.where(
        region == 0, near - 1, jnp.where(is_root, roots - 1, roots)
    ) + hands_on.astype(jnp.int32)

    if regions > 1:

        @pl.loop(0, greeted)
        def _(i):
            apart = (region + outward(i, regions) + regions) % regions
            giver = jnp.where(region < near, 0, region - stride)
            peer = jnp.where(is_root, apart, giver)
            pl.semaphore_signal(barrier, inc=1, device_id=(peer, tile), device_id_type=MESH)

    def greet(_, peer):
        pl.semaphore_signal(barrier, inc=1, device_id=(region, peer), device_id_type=MESH)

    peers(greet)
    for load in loads:
        load.start()
    for load in loads[:3]:
        load.wait()

    lane = iota((atm_blocks, cells), 1)
    level = lane // columns
    level_weight = jnp.zeros((atm_blocks, cells), F32)
    for l in range(cap):
        level_weight = jnp.where(level == l, weights_ref[l], level_weight)
    pieces = []
    for f in range(nf):
        x = atm_ref[:, f * cells : (f + 1) * cells].astype(F32) * level_weight
        x = x + pltpu.roll(x, 2 * columns, 1)
        pieces.append(x + pltpu.roll(x, columns, 1))
    combined = jnp.concatenate(pieces, axis=1)
    block = iota((atm_blocks, nf * cells), 1) % cells // columns
    stacked = jnp.concatenate([jnp.where(block == c, combined, 0.0) for c in range(cap)], axis=0)
    first, second = two_parts(stacked)
    third = (stacked - first.astype(F32) - second.astype(F32)).astype(BF16)
    table = jnp.concatenate([first, second, third], axis=0)
    width = 3 * cap * atm_blocks
    at = iota((width, tiles), 0)
    wanted = jnp.full((width, tiles), -1, jnp.int32)
    for c in range(cap):
        wanted = jnp.where(at // atm_blocks % cap == c, src_ref[0, c : c + 1, :], wanted)
    pick = jnp.where(wanted == at % atm_blocks, 1.0, 0.0).astype(BF16)
    packed = dot(pick, table, ((0,), (0,)))
    early, late = len(EARLY), len(LATE)
    early_rows, late_rows = (0, early), (LATE_ROW, late)
    for start, fields in ((0, EARLY), (LATE_ROW, LATE)):
        for n, f in enumerate(fields):
            send1[:, start + n, :] = packed[:, f * cells : (f + 1) * cells]

    at = iota((tiles, slots), 1)
    sender = chip_at(at // 8, -1) * 2 + at % 2
    repeat = jnp.where(sender == iota((tiles, slots), 0), 1.0, 0.0)
    by_slot = dot(owner_ref[0].astype(F32).astype(BF16), repeat.astype(BF16))
    own_row = iota((cap, slots), 0) == iota((cap, slots), 1) % 8 // 2
    owner_of = jnp.sum(jnp.where(own_row, by_slot, 0.0), axis=0, keepdims=True)
    feeds = jnp.where(
        owner_of.astype(jnp.int32) == iota((ocean_blocks, slots), 0), 1.0, 0.0
    ).astype(BF16)

    for rows in (early_rows, late_rows):
        recv1[pl.ds(tile, 1), pl.ds(*rows), :] = send1[pl.ds(tile, 1), pl.ds(*rows), :]

    pl.semaphore_wait(barrier, tiles - 1 + (reached if regions > 1 else 0))

    def send(source, target, rows, send_sem, recv_sem, peer):
        pltpu.make_async_remote_copy(
            src_ref=source.at[peer, pl.ds(*rows)],
            dst_ref=target.at[tile, pl.ds(*rows)],
            send_sem=send_sem,
            recv_sem=recv_sem,
            device_id=(region, peer),
            device_id_type=MESH,
        ).start()

    def drain(buffer, count, rows, sem):
        whole = buffer.at[pl.ds(0, count), pl.ds(0, rows)]
        pltpu.make_async_copy(whole, whole, sem).wait()

    peers(lambda n, peer: send(send1, recv1, early_rows, send1_sem, recv1_sem.at[n], peer))
    peers(lambda n, peer: send(send1, recv1, late_rows, late_send_sem, late_recv_sem, peer))

    for load in loads[3:]:
        load.wait()

    row8 = iota((8, cells), 0)
    lane8 = iota((8, cells), 1)
    own_lanes = row8 // 2 == lane8 // columns
    even = row8 % 2 == 0
    diagonal = [own_lanes & even, own_lanes & (row8 % 2 == 1)]

    def group(g):
        return remap[pl.ds(pl.multiple_of(g * depth, depth), depth), :]

    def forward(k, start, rows_in, column):
        g = chip_at(k, -1)
        halves = []
        for h in range(2):
            rows = [
                jnp.where(
                    diagonal[h],
                    jnp.broadcast_to(recv1[g * 2 + h, pl.ds(start + f, 1), :], (8, cells)),
                    0.0,
                )
                for f in range(rows_in)
            ]
            halves.append(jnp.concatenate(rows, axis=0))
        high, low = two_parts(jnp.concatenate(halves, axis=1))
        w = group(g)
        out = dot(high, w) + dot(low, w)
        for f in range(rows_in):
            at = (column + f) * cells
            contrib[pl.ds(pl.multiple_of(k * 8, 8), 8), at : at + cells] = out[
                f * 8 : (f + 1) * 8
            ]

    def select(some, columns_in):
        high, low = two_parts(contrib[some, columns_in])
        return dot(feeds[:, some], high) + dot(feeds[:, some], low)

    early_columns, late_columns = slice(0, early * cells), slice(early * cells, nf * cells)
    for n in range(CLASSES):
        drain(recv1, 2 * per_class - (n == CLASSES - 1), early, recv1_sem.at[n])

        @pl.loop(n * per_class, (n + 1) * per_class, unroll=min(FORWARD_UNROLL, per_class))
        def _(k):
            forward(k, 0, early, 0)

        part = select(slice(n * per_class * 8, (n + 1) * per_class * 8), early_columns)
        if n == 0:
            total_ref[:, early_columns] = part
        else:
            total_ref[:, early_columns] += part

    place = {f: n for n, f in enumerate(EARLY + LATE)}

    def bottom_of(fields):
        return {f: total_ref[:, place[f] * cells : (place[f] + 1) * cells] for f in fields}

    bottom = bottom_of(EARLY)
    surface = [ocean_ref[:, f * cells : (f + 1) * cells] for f in range(4)]
    transfer, latent, fresh = freshwater_flux(bottom, surface)

    weighted = jnp.sum(area_ref[...] * fresh, axis=0, keepdims=True)
    total = jnp.sum(area_ref[...], axis=0, keepdims=True)
    half = cells // 2
    low_lanes = iota((1, cells), 1) < half
    sums = jnp.where(
        low_lanes, weighted + pltpu.roll(weighted, half, 1), total + pltpu.roll(total, half, 1)
    )
    zrows[pl.ds(region, 1), pl.ds(0, 1), :] = sums.reshape(1, 1, cells)

    def row_copy(source, target, send_sem, recv_sem, device):
        return pltpu.make_async_remote_copy(
            src_ref=source,
            dst_ref=target,
            send_sem=send_sem,
            recv_sem=recv_sem,
            device_id=device,
            device_id_type=MESH,
        )

    for r in range(roots):

        @pl.when(region != r)
        def _():
            row = zrows.at[region, pl.ds(0, 1)]
            row_copy(row, row, zsend_sem.at[r], zrecv_sem, (r, tile)).start()

    drain(recv1, tiles - 1, late, late_recv_sem)

    @pl.loop(0, chips, unroll=min(FORWARD_UNROLL, per_class))
    def _(k):
        forward(k, LATE_ROW, late, early)

    total_ref[:, late_columns] = select(slice(0, slots), late_columns)
    bottom.update(bottom_of(LATE))
    raw = fluxes(bottom, surface, transfer, latent, fresh)
    for f in range(nflx):
        if f != 6:
            ocean_out[:, f * cells : (f + 1) * cells] = raw[f]
    out_parts = [slice(0, 6 * cells), slice(7 * cells, nflx * cells), slice(6 * cells, 7 * cells)]
    stores = [
        pltpu.make_async_copy(ocean_out.at[:, p], ocean_hbm_out.at[:, p], out_sem.at[n])
        for n, p in enumerate(out_parts)
    ] + [pltpu.make_async_copy(atm_out, atm_hbm_out, out_sem.at[3])]
    stores[0].start()
    stores[1].start()
    fresh_high, fresh_low = two_parts(fresh)
    fields = [r.astype(BF16) for r in raw]
    fields[6] = fresh_high
    rows_back[...] = dot(feeds, jnp.concatenate(fields + [fresh_low], axis=1), ((0,), (0,)))
    ones = jnp.ones((8, cells), F32)

    def pair(a, b):
        upper = row8 < 4
        return jnp.where(upper, a, b) + pltpu.roll(jnp.where(upper, b, a), 4, 0)

    def four(a, b):
        near = row8 % 4 < 2
        x = jnp.where(near, b, a)
        return jnp.where(near, a, b) + jnp.where(near, pltpu.roll(x, 6, 0), pltpu.roll(x, 2, 0))

    def backward(k):
        g = chip_at(k, -1)
        at_rows = pl.ds(pl.multiple_of(k * 8, 8), 8)
        rows = [rows_back[at_rows, f * cells : (f + 1) * cells] for f in range(nflx + 1)]
        left = jnp.concatenate(rows + [ones], axis=0).astype(BF16)
        out = dot(left, group(g), ((1,), (1,)))
        x = []
        for f in range(nflx + 1):
            piece = out[f * 8 : (f + 1) * 8]
            mixed = jnp.where(even, piece[:, :cells], piece[:, cells:])
            x.append(jnp.where(own_lanes, mixed, 0.0))
        x[6] = x[6] + x[nflx]
        q0 = four(pair(x[0], x[4]), pair(x[2], x[6]))
        q1 = four(pair(x[1], x[5]), pair(x[3], x[7]))
        send2[g * 2, pl.ds(0, 8), :] = jnp.where(even, q0, pltpu.roll(q1, 1, 0))
        send2[g * 2 + 1, pl.ds(0, 8), :] = jnp.where(even, pltpu.roll(q0, 7, 0), q1)
        for h in range(2):
            at = (nflx + 1) * 8
            send2[g * 2 + h, pl.ds(nflx, 1), :] = out[at : at + 1, h * cells : (h + 1) * cells]

    def send_back(k):
        chip = chip_at(k, -1)
        for peer in (chip * 2 + core, chip * 2 + 1 - core):
            send(send2, recv2, (0, nflx + 1), send2_sem, recv2_sem, peer)

    whole_steps = (chips - 1) // BACK_STEP

    @pl.loop(0, whole_steps)
    def _(i):
        for u in range(BACK_STEP):
            backward(i * BACK_STEP + u)
        for u in range(BACK_STEP):
            send_back(i * BACK_STEP + u)

    for k in range(whole_steps * BACK_STEP, chips):
        backward(k)
    for k in range(whole_steps * BACK_STEP, chips - 1):
        send_back(k)
    send(send2, recv2, (0, nflx + 1), send2_sem, recv2_sem, my_chip * 2 + 1 - core)
    recv2[pl.ds(tile, 1), pl.ds(0, nflx + 1), :] = send2[pl.ds(tile, 1), pl.ds(0, nflx + 1), :]

    @pl.when(is_root)
    def _():
        if regions > 1:
            drain(zrows, regions - 1, 1, zrecv_sem)
        column = jnp.sum(zrows[:, 0, :], axis=0, keepdims=True)
        trows[pl.ds(tile, 1), pl.ds(0, 1), :] = column.reshape(1, 1, cells)

        def send_sums(_, peer):
            row = trows.at[tile, pl.ds(0, 1)]
            row_copy(row, row, tsend_sem, trecv_sem, (region, peer)).start()

        peers(send_sums)

    drain(recv2, tiles - 1, nflx + 1, recv2_sem)
    lane_group = iota((atm_blocks, cells), 1) // columns

    def gather(rows):
        found = dot(pick[: cap * atm_blocks], jnp.concatenate(rows, axis=1).astype(BF16))
        outs = []
        for n in range(len(rows)):
            x = jnp.zeros((atm_blocks, cells), F32)
            for c in range(cap):
                x = jnp.where(
                    lane_group == c,
                    found[c * atm_blocks : (c + 1) * atm_blocks, n * cells : (n + 1) * cells],
                    x,
                )
            x = x + pltpu.roll(x, 2 * columns, 1)
            outs.append(x + pltpu.roll(x, columns, 1))
        return outs

    outs = gather([recv2[:, f, :] for f in range(nflx) if f != 6])
    outs.insert(6, None)

    @pl.when(is_root)
    def _():
        drain(trows, tiles - 1, 1, trecv_sem)
        everything = jnp.sum(trows[:, 0, :], axis=0, keepdims=True)
        zmean[1, pl.ds(0, 1), :] = everything

    if regions > roots:

        @pl.when(jnp.logical_not(is_root))
        def _():
            drain(zmean, 1, 1, mrecv_sem)

        def send_mean(peer):
            mean = zmean.at[1, pl.ds(0, 1)]
            row_copy(mean, mean, msend_sem, mrecv_sem, (peer, tile)).start()

        @pl.when(region == 0)
        def _():
            @pl.loop(roots, near)
            def _(r):
                send_mean(r)

        @pl.when(hands_on)
        def _():
            send_mean(region + stride)

    sums_all = zmean[1, pl.ds(0, 1), :]
    weighted_all = jnp.sum(jnp.where(low_lanes, sums_all, 0.0), axis=1, keepdims=True)
    area_all = jnp.sum(jnp.where(low_lanes, 0.0, sums_all), axis=1, keepdims=True)
    shift = weighted_all / area_all
    ocean_out[:, 6 * cells : 7 * cells] = fresh - shift
    stores[2].start()
    outs[6] = gather([recv2[:, 6, :] - shift * recv2[:, nflx, :]])[0]
    for t in range(nflx // cap):
        x = outs[t * cap]
        for c in range(1, cap):
            x = jnp.where(lane_group == c, outs[t * cap + c], x)
        atm_out[:, t * cells : (t + 1) * cells] = x
    stores[3].start()

    drain(send1, tiles - 1, early, send1_sem)
    drain(send1, tiles - 1, late, late_send_sem)
    drain(send2, tiles - 1, nflx + 1, send2_sem)
    for r in range(roots):

        @pl.when(region != r)
        def _():
            drain(zrows, 1, 1, zsend_sem.at[r])

    @pl.when(is_root)
    def _():
        drain(trows, tiles - 1, 1, tsend_sem)

    if regions > roots:
        if near > roots:

            @pl.when(region == 0)
            def _():
                drain(zrows, near - roots, 1, msend_sem)

        @pl.when(hands_on)
        def _():
            drain(zrows, 1, 1, msend_sem)

    for store in stores:
        store.wait()


def copy_out(ocean_in, atm_in, ocean_out, atm_out, ocean_held, atm_held, sem):
    def both(first, second):
        copies = [
            pltpu.make_async_copy(source, target, sem.at[n])
            for n, (source, target) in enumerate(zip(first, second))
        ]
        for copy in copies:
            copy.start()
        for copy in copies:
            copy.wait()

    held = (ocean_held, atm_held)
    both((ocean_in, atm_in), held)
    both(held, (ocean_out, atm_out))


def per_device(
    regions, tiles, atm_state, ocean_state, cell_area, level_weights, remap, send_src, recv_ocn
):
    cap = send_src.shape[2]
    slots = tiles * cap
    atm_blocks = atm_state.shape[0]
    ocean_blocks, cells = cell_area.shape
    columns = remap.shape[1]
    nf = atm_state.shape[1] // cells
    nflx = 8
    hbm = pl.BlockSpec(memory_space=pl.ANY)
    box = pltpu.VMEM((tiles, 16, cells), F32)
    dma = pltpu.SemaphoreType.DMA
    results = (
        jax.ShapeDtypeStruct((ocean_blocks, nflx * cells), F32),
        jax.ShapeDtypeStruct((atm_blocks, nflx * columns), F32),
    )
    made = pl.pallas_call(
        functools.partial(kernel, regions, tiles),
        out_shape=results,
        in_specs=[hbm, hbm, hbm, pl.BlockSpec(memory_space=pltpu.SMEM), hbm, hbm, hbm],
        out_specs=(hbm, hbm),
        scratch_shapes=[
            pltpu.VMEM(atm_state.shape, BF16),
            pltpu.VMEM(ocean_state.shape, F32),
            pltpu.VMEM(cell_area.shape, F32),
            pltpu.VMEM((1, cap, tiles), jnp.int32),
            pltpu.VMEM((1, cap, tiles), jnp.int32),
            pltpu.VMEM(results[0].shape, F32),
            pltpu.VMEM(results[1].shape, F32),
            pltpu.VMEM((slots * columns, cells), BF16),
            box,
            box,
            pltpu.VMEM((slots, nf * cells), F32),
            pltpu.VMEM((ocean_blocks, nf * cells), F32),
            pltpu.VMEM((slots, (nflx + 1) * cells), F32),
            box,
            box,
            pltpu.VMEM((tiles, 8, cells), F32),
            pltpu.VMEM((regions, 8, cells), F32),
            pltpu.VMEM((2, 8, cells), F32),
            pltpu.SemaphoreType.DMA((6,)),
            dma,
            pltpu.SemaphoreType.DMA((CLASSES,)),
            dma, dma, dma, dma,
            pltpu.SemaphoreType.DMA((ROOTS,)),
            dma, dma, dma, dma, dma,
            pltpu.SemaphoreType.DMA((4,)),
        ],
        compiler_params=pltpu.CompilerParams(
            collective_id=0, has_side_effects=True, vmem_limit_bytes=60 * 1024 * 1024
        ),
        cost_estimate=pl.CostEstimate(
            flops=400_000_000, bytes_accessed=4_000_000, transcendentals=100_000
        ),
        name="couple",
    )(
        atm_state, ocean_state, cell_area, level_weights,
        remap.reshape(slots * columns, cells),
        jnp.swapaxes(send_src, 1, 2), jnp.swapaxes(recv_ocn, 1, 2),
    )
    return pl.pallas_call(
        copy_out,
        out_shape=results,
        in_specs=[hbm, hbm],
        out_specs=(hbm, hbm),
        scratch_shapes=[
            pltpu.VMEM(results[0].shape, F32),
            pltpu.VMEM(results[1].shape, F32),
            pltpu.SemaphoreType.DMA((2,)),
        ],
        compiler_params=pltpu.CompilerParams(vmem_limit_bytes=60 * 1024 * 1024),
        name="results",
    )(*made)


def solution(mesh):
    in_specs = (
        P(("region", "tile"), None),
        P(("region", "tile"), None),
        P(("region", "tile"), None),
        P(),
        P(("region", "tile"), None, None),
        P(("region", "tile"), None, None),
        P(("region", "tile"), None, None),
    )
    out_specs = (P(("region", "tile"), None), P(("region", "tile"), None))
    return jax.shard_map(
        functools.partial(per_device, mesh.shape["region"], mesh.shape["tile"]),
        mesh=mesh,
        in_specs=in_specs,
        out_specs=out_specs,
        check_vma=False,
    )
```

```python
import functools

import jax
import jax.numpy as jnp
from jax import lax
from jax.experimental import pallas as pl
from jax.experimental.pallas import tpu as pltpu
from jax.sharding import PartitionSpec as P

F32 = jnp.float32
BF16 = jnp.bfloat16
MESH = pl.DeviceIdType.MESH
CLASSES = 4
FORWARD_UNROLL = 4
BACK_STEP = 4
ROOTS = 2
EARLY = (0, 1, 3, 6, 7, 8, 9)
LATE = (2, 4, 5)
STEPS = 32766.0
LATE_ROW = 4


def iota(shape, axis):
    return lax.broadcasted_iota(jnp.int32, shape, axis)


def two_parts(x):
    high = x.astype(BF16)
    return high, (x - high.astype(F32)).astype(BF16)


def dot(a, b, contract=((1,), (0,))):
    return lax.dot_general(a, b, (contract, ((), ())), preferred_element_type=F32)


def softplus(x):
    return jnp.maximum(x, 0.0) + jnp.log1p(jnp.exp(-jnp.abs(x)))


def freshwater_flux(bottom, surface):
    sst, ocean_u, ocean_v, _ = surface
    wind_x = bottom[0] - ocean_u
    wind_y = bottom[1] - ocean_v
    speed = jnp.sqrt(wind_x * wind_x + wind_y * wind_y + bottom[9] * bottom[9] + 1.0)
    transfer = 0.1 * jnp.exp(0.2 * jnp.tanh(bottom[8])) * speed
    saturated = jnp.exp(0.1 * sst - 0.1 * jnp.tanh(bottom[7]))
    latent = transfer * (bottom[3] - saturated)
    return transfer, latent, softplus(bottom[6]) + latent


def fluxes(bottom, surface, transfer, latent, freshwater):
    sst, ocean_u, ocean_v, albedo_in = surface
    stress_x = transfer * (bottom[0] - ocean_u)
    stress_y = transfer * (bottom[1] - ocean_v)
    sensible = transfer * (bottom[2] - sst)
    albedo = 0.05 + 0.3 * (1.0 / (1.0 + jnp.exp(-albedo_in)))
    shortwave = (1.0 - albedo) * softplus(bottom[4])
    longwave = softplus(bottom[5]) - 1.0 - 0.2 * sst
    heating = sensible + latent + shortwave + longwave
    return [stress_x, stress_y, sensible, latent, shortwave, longwave, freshwater, heating]


def chip_grid(tiles):
    chips = tiles // 2
    height = min(8, chips)
    return chips // height, height


def outward(k, size):
    step = (k + 1) // 2
    return size // 2 + step * (1 - 2 * (k % 2))


def kernel(
    regions, tiles, atm_hbm, ocean_hbm, area_hbm, weights_ref, remap_hbm, src_hbm, owner_hbm,
    ocean_hbm_out, atm_hbm_out,
    atm_ref, ocean_ref, area_ref, src_ref, owner_ref, ocean_out, atm_out,
    remap, send1, recv1, contrib, total_ref, rows_back, send2, recv2, trows, zrows, zmean,
    load_sem, send1_sem, recv1_sem, send2_sem, recv2_sem, tsend_sem, trecv_sem, zsend_sem, zrecv_sem,
    msend_sem, mrecv_sem, late_send_sem, late_recv_sem, out_sem,
):
    region = lax.axis_index("region")
    tile = lax.axis_index("tile")
    cap = src_ref.shape[1]
    atm_blocks = atm_ref.shape[0]
    ocean_blocks, cells = area_ref.shape
    nf = atm_ref.shape[1] // cells
    columns = cells // cap
    slots = tiles * cap
    nflx = 8
    wide, high_grid = chip_grid(tiles)
    chips = tiles // 2
    per_class = chips // CLASSES
    depth = 8 * columns

    loads = [
        pltpu.make_async_copy(source, target, load_sem.at[n])
        for n, (source, target) in enumerate(
            [
                (atm_hbm, atm_ref),
                (src_hbm, src_ref),
                (owner_hbm, owner_ref),
                (ocean_hbm, ocean_ref),
                (area_hbm, area_ref),
                (remap_hbm, remap),
            ]
        )
    ]

    barrier = pltpu.get_barrier_semaphore()
    my_chip = tile // 2
    core = tile % 2

    def chip_at(k, sign):
        away_y = outward(k // wide, high_grid)
        away_x = outward(k % wide, wide)
        x = (my_chip // high_grid + sign * away_x + wide) % wide
        y = (my_chip % high_grid + sign * away_y + high_grid) % high_grid
        return x * high_grid + y

    def peers(visit):
        for n in range(CLASSES):

            @pl.loop(n * per_class, min((n + 1) * per_class, chips - 1))
            def _(k):
                chip = chip_at(k, 1)
                visit(n, chip * 2 + core)
                visit(n, chip * 2 + 1 - core)

        visit(CLASSES - 1, my_chip * 2 + 1 - core)

    roots = min(ROOTS, regions)
    near, stride = max(regions // 2, roots), regions // 4
    is_root = region < roots
    hands_on = (region >= near - stride) & (region < regions - stride) & (near < regions)
    greeted = jnp.where(is_root, regions - 1, 1)
    teller = roots - 1
    reached = jnp.where(
        is_root, jnp.where(region == teller, near - 1, roots - 1), roots
    ) + hands_on.astype(jnp.int32)

    if regions > 1:

        @pl.loop(0, greeted)
        def _(i):
            apart = (region + outward(i, regions) + regions) % regions
            giver = jnp.where(region < near, teller, region - stride)
            peer = jnp.where(is_root, apart, giver)
            pl.semaphore_signal(barrier, inc=1, device_id=(peer, tile), device_id_type=MESH)

    def greet(_, peer):
        pl.semaphore_signal(barrier, inc=1, device_id=(region, peer), device_id_type=MESH)

    peers(greet)
    for load in loads:
        load.start()
    for load in loads[:3]:
        load.wait()

    lane = iota((atm_blocks, cells), 1)
    level = lane // columns
    level_weight = jnp.zeros((atm_blocks, cells), F32)
    for l in range(cap):
        level_weight = jnp.where(level == l, weights_ref[l], level_weight)
    pieces = []
    for f in range(nf):
        x = atm_ref[:, f * cells : (f + 1) * cells].astype(F32) * level_weight
        x = x + pltpu.roll(x, 2 * columns, 1)
        pieces.append(x + pltpu.roll(x, columns, 1))
    combined = jnp.concatenate(pieces, axis=1)
    block = iota((atm_blocks, nf * cells), 1) % cells // columns
    stacked = jnp.concatenate([jnp.where(block == c, combined, 0.0) for c in range(cap)], axis=0)
    first, second = two_parts(stacked)
    third = (stacked - first.astype(F32) - second.astype(F32)).astype(BF16)
    table = jnp.concatenate([first, second, third], axis=0)
    width = 3 * cap * atm_blocks
    at = iota((width, tiles), 0)
    wanted = jnp.full((width, tiles), -1, jnp.int32)
    for c in range(cap):
        wanted = jnp.where(at // atm_blocks % cap == c, src_ref[0, c : c + 1, :], wanted)
    pick = jnp.where(wanted == at % atm_blocks, 1.0, 0.0).astype(BF16)
    packed = dot(pick, table, ((0,), (0,)))
    early, late = len(EARLY), len(LATE)
    early_words, late_words = early // 2 + 1, late // 2 + 1
    early_rows, late_rows = (0, early_words), (LATE_ROW, late_words)
    largest = jnp.max(jnp.abs(combined), axis=1, keepdims=True)
    largest = jnp.max(largest, axis=0, keepdims=True)
    power = jnp.floor(jnp.log2(jnp.maximum(largest, 1e-30))) + 1.0
    whole = jnp.floor(packed * (STEPS * jnp.exp2(-power)) + 0.5).astype(jnp.int32)
    power = jnp.broadcast_to(power.astype(jnp.int32), (tiles, cells))
    for start, fields in ((0, EARLY), (LATE_ROW, LATE)):
        parts_of = [whole[:, f * cells : (f + 1) * cells] for f in fields] + [power]
        for n in range(len(parts_of) // 2):
            send1[:, start + n, :] = parts_of[2 * n] * 65536 + (parts_of[2 * n + 1] + 32768)

    at = iota((tiles, slots), 1)
    sender = chip_at(at // 8, -1) * 2 + at % 2
    repeat = jnp.where(sender == iota((tiles, slots), 0), 1.0, 0.0)
    by_slot = dot(owner_ref[0].astype(F32).astype(BF16), repeat.astype(BF16))
    own_row = iota((cap, slots), 0) == iota((cap, slots), 1) % 8 // 2
    owner_of = jnp.sum(jnp.where(own_row, by_slot, 0.0), axis=0, keepdims=True)
    feeds = jnp.where(
        owner_of.astype(jnp.int32) == iota((ocean_blocks, slots), 0), 1.0, 0.0
    ).astype(BF16)

    for rows in (early_rows, late_rows):
        recv1[pl.ds(tile, 1), pl.ds(*rows), :] = send1[pl.ds(tile, 1), pl.ds(*rows), :]

    pl.semaphore_wait(barrier, tiles - 1 + (reached if regions > 1 else 0))

    def send(source, target, rows, send_sem, recv_sem, peer):
        pltpu.make_async_remote_copy(
            src_ref=source.at[peer, pl.ds(*rows)],
            dst_ref=target.at[tile, pl.ds(*rows)],
            send_sem=send_sem,
            recv_sem=recv_sem,
            device_id=(region, peer),
            device_id_type=MESH,
        ).start()

    def drain(buffer, count, rows, sem):
        whole = buffer.at[pl.ds(0, count), pl.ds(0, rows)]
        pltpu.make_async_copy(whole, whole, sem).wait()

    peers(lambda n, peer: send(send1, recv1, early_rows, send1_sem, recv1_sem.at[n], peer))
    peers(lambda n, peer: send(send1, recv1, late_rows, late_send_sem, late_recv_sem.at[n], peer))

    for load in loads[3:]:
        load.wait()

    row8 = iota((8, cells), 0)
    lane8 = iota((8, cells), 1)
    own_lanes = row8 // 2 == lane8 // columns
    even = row8 % 2 == 0
    diagonal = [own_lanes & even, own_lanes & (row8 % 2 == 1)]

    def group(g):
        return remap[pl.ds(pl.multiple_of(g * depth, depth), depth), :]

    def forward(k, start, rows_in, column):
        g = chip_at(k, -1)
        halves = []
        for h in range(2):
            values = []
            for n in range(rows_in // 2 + 1):
                word = recv1[g * 2 + h, pl.ds(start + n, 1), :]
                values += [word >> 16, (word & 65535) - 32768]
            scale = jnp.exp2(values[rows_in].astype(F32)) * (1.0 / STEPS)
            rows = [
                jnp.where(
                    diagonal[h],
                    jnp.broadcast_to(value.astype(F32) * scale, (8, cells)),
                    0.0,
                )
                for value in values[:rows_in]
            ]
            halves.append(jnp.concatenate(rows, axis=0))
        high, low = two_parts(jnp.concatenate(halves, axis=1))
        w = group(g)
        out = dot(high, w) + dot(low, w)
        for f in range(rows_in):
            at = (column + f) * cells
            contrib[pl.ds(pl.multiple_of(k * 8, 8), 8), at : at + cells] = out[
                f * 8 : (f + 1) * 8
            ]

    def select(some, columns_in):
        high, low = two_parts(contrib[some, columns_in])
        return dot(feeds[:, some], high) + dot(feeds[:, some], low)

    early_columns, late_columns = slice(0, early * cells), slice(early * cells, nf * cells)
    for n in range(CLASSES):
        drain(recv1, 2 * per_class - (n == CLASSES - 1), early_words, recv1_sem.at[n])

        @pl.loop(n * per_class, (n + 1) * per_class, unroll=min(FORWARD_UNROLL, per_class))
        def _(k):
            forward(k, 0, early, 0)

        part = select(slice(n * per_class * 8, (n + 1) * per_class * 8), early_columns)
        if n == 0:
            total_ref[:, early_columns] = part
        else:
            total_ref[:, early_columns] += part

    place = {f: n for n, f in enumerate(EARLY + LATE)}

    def bottom_of(fields):
        return {f: total_ref[:, place[f] * cells : (place[f] + 1) * cells] for f in fields}

    bottom = bottom_of(EARLY)
    surface = [ocean_ref[:, f * cells : (f + 1) * cells] for f in range(4)]
    transfer, latent, fresh = freshwater_flux(bottom, surface)

    weighted = jnp.sum(area_ref[...] * fresh, axis=0, keepdims=True)
    total = jnp.sum(area_ref[...], axis=0, keepdims=True)
    half = cells // 2
    low_lanes = iota((1, cells), 1) < half
    sums = jnp.where(
        low_lanes, weighted + pltpu.roll(weighted, half, 1), total + pltpu.roll(total, half, 1)
    )
    zrows[pl.ds(region, 1), pl.ds(0, 1), :] = sums.reshape(1, 1, cells)

    def row_copy(source, target, send_sem, recv_sem, device):
        return pltpu.make_async_remote_copy(
            src_ref=source,
            dst_ref=target,
            send_sem=send_sem,
            recv_sem=recv_sem,
            device_id=device,
            device_id_type=MESH,
        )

    for r in range(roots):

        @pl.when(region != r)
        def _():
            row = zrows.at[region, pl.ds(0, 1)]
            row_copy(row, row, zsend_sem.at[r], zrecv_sem, (r, tile)).start()

    for n in range(CLASSES):
        drain(recv1, 2 * per_class - (n == CLASSES - 1), late_words, late_recv_sem.at[n])

        @pl.loop(n * per_class, (n + 1) * per_class, unroll=min(FORWARD_UNROLL, per_class))
        def _(k):
            forward(k, LATE_ROW, late, early)

    total_ref[:, late_columns] = select(slice(0, slots), late_columns)
    bottom.update(bottom_of(LATE))
    raw = fluxes(bottom, surface, transfer, latent, fresh)
    for f in range(nflx):
        if f != 6:
            ocean_out[:, f * cells : (f + 1) * cells] = raw[f]
    out_parts = [slice(0, 6 * cells), slice(7 * cells, nflx * cells), slice(6 * cells, 7 * cells)]
    stores = [
        pltpu.make_async_copy(ocean_out.at[:, p], ocean_hbm_out.at[:, p], out_sem.at[n])
        for n, p in enumerate(out_parts)
    ] + [pltpu.make_async_copy(atm_out, atm_hbm_out, out_sem.at[3])]
    stores[0].start()
    stores[1].start()
    fresh_high, fresh_low = two_parts(fresh)
    fields = [r.astype(BF16) for r in raw]
    fields[6] = fresh_high
    rows_back[...] = dot(feeds, jnp.concatenate(fields + [fresh_low], axis=1), ((0,), (0,)))
    ones = jnp.ones((8, cells), F32)

    def pair(a, b):
        upper = row8 < 4
        return jnp.where(upper, a, b) + pltpu.roll(jnp.where(upper, b, a), 4, 0)

    def four(a, b):
        near = row8 % 4 < 2
        x = jnp.where(near, b, a)
        return jnp.where(near, a, b) + jnp.where(near, pltpu.roll(x, 6, 0), pltpu.roll(x, 2, 0))

    def backward(k):
        g = chip_at(k, -1)
        at_rows = pl.ds(pl.multiple_of(k * 8, 8), 8)
        rows = [rows_back[at_rows, f * cells : (f + 1) * cells] for f in range(nflx + 1)]
        left = jnp.concatenate(rows + [ones], axis=0).astype(BF16)
        out = dot(left, group(g), ((1,), (1,)))
        x = []
        for f in range(nflx + 1):
            piece = out[f * 8 : (f + 1) * 8]
            mixed = jnp.where(even, piece[:, :cells], piece[:, cells:])
            x.append(jnp.where(own_lanes, mixed, 0.0))
        x[6] = x[6] + x[nflx]
        q0 = four(pair(x[0], x[4]), pair(x[2], x[6]))
        q1 = four(pair(x[1], x[5]), pair(x[3], x[7]))
        send2[g * 2, pl.ds(0, 8), :] = jnp.where(even, q0, pltpu.roll(q1, 1, 0))
        send2[g * 2 + 1, pl.ds(0, 8), :] = jnp.where(even, pltpu.roll(q0, 7, 0), q1)
        for h in range(2):
            at = (nflx + 1) * 8
            send2[g * 2 + h, pl.ds(nflx, 1), :] = out[at : at + 1, h * cells : (h + 1) * cells]

    def send_back(k):
        chip = chip_at(k, -1)
        for peer in (chip * 2 + core, chip * 2 + 1 - core):
            send(send2, recv2, (0, nflx + 1), send2_sem, recv2_sem, peer)

    whole_steps = (chips - 1) // BACK_STEP

    @pl.loop(0, whole_steps)
    def _(i):
        for u in range(BACK_STEP):
            backward(i * BACK_STEP + u)
        for u in range(BACK_STEP):
            send_back(i * BACK_STEP + u)

    for k in range(whole_steps * BACK_STEP, chips):
        backward(k)
    for k in range(whole_steps * BACK_STEP, chips - 1):
        send_back(k)
    send(send2, recv2, (0, nflx + 1), send2_sem, recv2_sem, my_chip * 2 + 1 - core)
    recv2[pl.ds(tile, 1), pl.ds(0, nflx + 1), :] = send2[pl.ds(tile, 1), pl.ds(0, nflx + 1), :]

    @pl.when(is_root)
    def _():
        if regions > 1:
            drain(zrows, regions - 1, 1, zrecv_sem)
        column = jnp.sum(zrows[:, 0, :], axis=0, keepdims=True)
        trows[pl.ds(tile, 1), pl.ds(0, 1), :] = column.reshape(1, 1, cells)

        def send_sums(_, peer):
            row = trows.at[tile, pl.ds(0, 1)]
            row_copy(row, row, tsend_sem, trecv_sem, (region, peer)).start()

        peers(send_sums)

    drain(recv2, tiles - 1, nflx + 1, recv2_sem)
    lane_group = iota((atm_blocks, cells), 1) // columns

    def gather(rows):
        found = dot(pick[: cap * atm_blocks], jnp.concatenate(rows, axis=1).astype(BF16))
        outs = []
        for n in range(len(rows)):
            x = jnp.zeros((atm_blocks, cells), F32)
            for c in range(cap):
                x = jnp.where(
                    lane_group == c,
                    found[c * atm_blocks : (c + 1) * atm_blocks, n * cells : (n + 1) * cells],
                    x,
                )
            x = x + pltpu.roll(x, 2 * columns, 1)
            outs.append(x + pltpu.roll(x, columns, 1))
        return outs

    outs = gather([recv2[:, f, :] for f in range(nflx) if f != 6])
    outs.insert(6, None)

    @pl.when(is_root)
    def _():
        drain(trows, tiles - 1, 1, trecv_sem)
        everything = jnp.sum(trows[:, 0, :], axis=0, keepdims=True)
        zmean[1, pl.ds(0, 1), :] = everything

    if regions > roots:

        @pl.when(jnp.logical_not(is_root))
        def _():
            drain(zmean, 1, 1, mrecv_sem)

        def send_mean(peer):
            mean = zmean.at[1, pl.ds(0, 1)]
            row_copy(mean, mean, msend_sem, mrecv_sem, (peer, tile)).start()

        @pl.when(region == teller)
        def _():
            @pl.loop(roots, near)
            def _(r):
                send_mean(r)

        @pl.when(hands_on)
        def _():
            send_mean(region + stride)

    sums_all = zmean[1, pl.ds(0, 1), :]
    weighted_all = jnp.sum(jnp.where(low_lanes, sums_all, 0.0), axis=1, keepdims=True)
    area_all = jnp.sum(jnp.where(low_lanes, 0.0, sums_all), axis=1, keepdims=True)
    shift = weighted_all / area_all
    ocean_out[:, 6 * cells : 7 * cells] = fresh - shift
    stores[2].start()
    outs[6] = gather([recv2[:, 6, :] - shift * recv2[:, nflx, :]])[0]
    for t in range(nflx // cap):
        x = outs[t * cap]
        for c in range(1, cap):
            x = jnp.where(lane_group == c, outs[t * cap + c], x)
        atm_out[:, t * cells : (t + 1) * cells] = x
    stores[3].start()

    drain(send1, tiles - 1, early_words, send1_sem)
    drain(send1, tiles - 1, late_words, late_send_sem)
    drain(send2, tiles - 1, nflx + 1, send2_sem)
    for r in range(roots):

        @pl.when(region != r)
        def _():
            drain(zrows, 1, 1, zsend_sem.at[r])

    @pl.when(is_root)
    def _():
        drain(trows, tiles - 1, 1, tsend_sem)

    if regions > roots:
        if near > roots:

            @pl.when(region == teller)
            def _():
                drain(zrows, near - roots, 1, msend_sem)

        @pl.when(hands_on)
        def _():
            drain(zrows, 1, 1, msend_sem)

    for store in stores:
        store.wait()


def copy_out(ocean_in, atm_in, ocean_out, atm_out, ocean_held, atm_held, sem):
    def both(first, second):
        copies = [
            pltpu.make_async_copy(source, target, sem.at[n])
            for n, (source, target) in enumerate(zip(first, second))
        ]
        for copy in copies:
            copy.start()
        for copy in copies:
            copy.wait()

    held = (ocean_held, atm_held)
    both((ocean_in, atm_in), held)
    both(held, (ocean_out, atm_out))


def per_device(
    regions, tiles, atm_state, ocean_state, cell_area, level_weights, remap, send_src, recv_ocn
):
    cap = send_src.shape[2]
    slots = tiles * cap
    atm_blocks = atm_state.shape[0]
    ocean_blocks, cells = cell_area.shape
    columns = remap.shape[1]
    nf = atm_state.shape[1] // cells
    nflx = 8
    hbm = pl.BlockSpec(memory_space=pl.ANY)
    box = pltpu.VMEM((tiles, 16, cells), F32)
    dma = pltpu.SemaphoreType.DMA
    results = (
        jax.ShapeDtypeStruct((ocean_blocks, nflx * cells), F32),
        jax.ShapeDtypeStruct((atm_blocks, nflx * columns), F32),
    )
    made = pl.pallas_call(
        functools.partial(kernel, regions, tiles),
        out_shape=results,
        in_specs=[hbm, hbm, hbm, pl.BlockSpec(memory_space=pltpu.SMEM), hbm, hbm, hbm],
        out_specs=(hbm, hbm),
        scratch_shapes=[
            pltpu.VMEM(atm_state.shape, BF16),
            pltpu.VMEM(ocean_state.shape, F32),
            pltpu.VMEM(cell_area.shape, F32),
            pltpu.VMEM((1, cap, tiles), jnp.int32),
            pltpu.VMEM((1, cap, tiles), jnp.int32),
            pltpu.VMEM(results[0].shape, F32),
            pltpu.VMEM(results[1].shape, F32),
            pltpu.VMEM((slots * columns, cells), BF16),
            pltpu.VMEM((tiles, 8, cells), jnp.int32),
            pltpu.VMEM((tiles, 8, cells), jnp.int32),
            pltpu.VMEM((slots, nf * cells), F32),
            pltpu.VMEM((ocean_blocks, nf * cells), F32),
            pltpu.VMEM((slots, (nflx + 1) * cells), F32),
            box,
            box,
            pltpu.VMEM((tiles, 8, cells), F32),
            pltpu.VMEM((regions, 8, cells), F32),
            pltpu.VMEM((2, 8, cells), F32),
            pltpu.SemaphoreType.DMA((6,)),
            dma,
            pltpu.SemaphoreType.DMA((CLASSES,)),
            dma, dma, dma, dma,
            pltpu.SemaphoreType.DMA((ROOTS,)),
            dma, dma, dma, dma,
            pltpu.SemaphoreType.DMA((CLASSES,)),
            pltpu.SemaphoreType.DMA((4,)),
        ],
        compiler_params=pltpu.CompilerParams(
            collective_id=0, has_side_effects=True, vmem_limit_bytes=60 * 1024 * 1024
        ),
        cost_estimate=pl.CostEstimate(
            flops=400_000_000, bytes_accessed=4_000_000, transcendentals=100_000
        ),
        name="couple",
    )(
        atm_state, ocean_state, cell_area, level_weights,
        remap.reshape(slots * columns, cells),
        jnp.swapaxes(send_src, 1, 2), jnp.swapaxes(recv_ocn, 1, 2),
    )
    return pl.pallas_call(
        copy_out,
        out_shape=results,
        in_specs=[hbm, hbm],
        out_specs=(hbm, hbm),
        scratch_shapes=[
            pltpu.VMEM(results[0].shape, F32),
            pltpu.VMEM(results[1].shape, F32),
            pltpu.SemaphoreType.DMA((2,)),
        ],
        compiler_params=pltpu.CompilerParams(vmem_limit_bytes=60 * 1024 * 1024),
        name="results",
    )(*made)


def solution(mesh):
    in_specs = (
        P(("region", "tile"), None),
        P(("region", "tile"), None),
        P(("region", "tile"), None),
        P(),
        P(("region", "tile"), None, None),
        P(("region", "tile"), None, None),
        P(("region", "tile"), None, None),
    )
    out_specs = (P(("region", "tile"), None), P(("region", "tile"), None))
    return jax.shard_map(
        functools.partial(per_device, mesh.shape["region"], mesh.shape["tile"]),
        mesh=mesh,
        in_specs=in_specs,
        out_specs=out_specs,
        check_vma=False,
    )
```

```python
import functools

import jax
import jax.numpy as jnp
from jax import lax
from jax.experimental import pallas as pl
from jax.experimental.pallas import tpu as pltpu
from jax.sharding import PartitionSpec as P

F32 = jnp.float32
BF16 = jnp.bfloat16
MESH = pl.DeviceIdType.MESH
CLASSES = 4
FORWARD_UNROLL = 4
BACK_STEP = 4
ROOTS = 2
PIECES = 4
EARLY = (0, 1, 3, 6, 7, 8, 9)
LATE = (2, 4, 5)
STEPS = 32766.0
LATE_ROW = 4


def iota(shape, axis):
    return lax.broadcasted_iota(jnp.int32, shape, axis)


def two_parts(x):
    high = x.astype(BF16)
    return high, (x - high.astype(F32)).astype(BF16)


def dot(a, b, contract=((1,), (0,))):
    return lax.dot_general(a, b, (contract, ((), ())), preferred_element_type=F32)


def softplus(x):
    return jnp.maximum(x, 0.0) + jnp.log1p(jnp.exp(-jnp.abs(x)))


def freshwater_flux(bottom, surface):
    sst, ocean_u, ocean_v, _ = surface
    wind_x = bottom[0] - ocean_u
    wind_y = bottom[1] - ocean_v
    speed = jnp.sqrt(wind_x * wind_x + wind_y * wind_y + bottom[9] * bottom[9] + 1.0)
    transfer = 0.1 * jnp.exp(0.2 * jnp.tanh(bottom[8])) * speed
    saturated = jnp.exp(0.1 * sst - 0.1 * jnp.tanh(bottom[7]))
    latent = transfer * (bottom[3] - saturated)
    return transfer, latent, softplus(bottom[6]) + latent


def fluxes(bottom, surface, transfer, latent, freshwater):
    sst, ocean_u, ocean_v, albedo_in = surface
    stress_x = transfer * (bottom[0] - ocean_u)
    stress_y = transfer * (bottom[1] - ocean_v)
    sensible = transfer * (bottom[2] - sst)
    albedo = 0.05 + 0.3 * (1.0 / (1.0 + jnp.exp(-albedo_in)))
    shortwave = (1.0 - albedo) * softplus(bottom[4])
    longwave = softplus(bottom[5]) - 1.0 - 0.2 * sst
    heating = sensible + latent + shortwave + longwave
    return [stress_x, stress_y, sensible, latent, shortwave, longwave, freshwater, heating]


def chip_grid(tiles):
    chips = tiles // 2
    height = min(8, chips)
    return chips // height, height


def outward(k, size):
    step = (k + 1) // 2
    return size // 2 + step * (1 - 2 * (k % 2))


def kernel(
    regions, tiles, atm_hbm, ocean_hbm, area_hbm, weights_ref, remap_hbm, src_hbm, owner_hbm,
    ocean_hbm_out, atm_hbm_out,
    atm_ref, ocean_ref, area_ref, src_ref, owner_ref, ocean_out, atm_out,
    remap, send1, recv1, contrib, total_ref, rows_back, send2, recv2, trows, zrows, zmean,
    load_sem, send1_sem, recv1_sem, send2_sem, recv2_sem, tsend_sem, trecv_sem, zsend_sem, zrecv_sem,
    msend_sem, mrecv_sem, late_send_sem, late_recv_sem, out_sem,
):
    region = lax.axis_index("region")
    tile = lax.axis_index("tile")
    cap = src_ref.shape[1]
    atm_blocks = atm_ref.shape[0]
    ocean_blocks, cells = area_ref.shape
    nf = atm_ref.shape[1] // cells
    columns = cells // cap
    slots = tiles * cap
    nflx = 8
    wide, high_grid = chip_grid(tiles)
    chips = tiles // 2
    per_class = chips // CLASSES
    depth = 8 * columns

    loads = [
        pltpu.make_async_copy(source, target, load_sem.at[n])
        for n, (source, target) in enumerate(
            [
                (atm_hbm, atm_ref),
                (src_hbm, src_ref),
                (owner_hbm, owner_ref),
                (ocean_hbm, ocean_ref),
                (area_hbm, area_ref),
                (remap_hbm, remap),
            ]
        )
    ]

    barrier = pltpu.get_barrier_semaphore()
    my_chip = tile // 2
    core = tile % 2

    def chip_at(k, sign):
        away_y = outward(k // wide, high_grid)
        away_x = outward(k % wide, wide)
        x = (my_chip // high_grid + sign * away_x + wide) % wide
        y = (my_chip % high_grid + sign * away_y + high_grid) % high_grid
        return x * high_grid + y

    def peers(visit):
        for n in range(CLASSES):

            @pl.loop(n * per_class, min((n + 1) * per_class, chips - 1))
            def _(k):
                chip = chip_at(k, 1)
                visit(n, chip * 2 + core)
                visit(n, chip * 2 + 1 - core)

        visit(CLASSES - 1, my_chip * 2 + 1 - core)

    roots = min(ROOTS, regions)
    near, stride = max(regions // 2, roots), regions // 4
    is_root = region < roots
    hands_on = (region >= near - stride) & (region < regions - stride) & (near < regions)
    greeted = jnp.where(is_root, regions - 1, 1)
    teller = roots - 1
    reached = jnp.where(
        is_root, jnp.where(region == teller, near - 1, roots - 1), roots
    ) + hands_on.astype(jnp.int32)

    if regions > 1:

        @pl.loop(0, greeted)
        def _(i):
            apart = (region + outward(i, regions) + regions) % regions
            giver = jnp.where(region < near, teller, region - stride)
            peer = jnp.where(is_root, apart, giver)
            pl.semaphore_signal(barrier, inc=1, device_id=(peer, tile), device_id_type=MESH)

    def greet(_, peer):
        pl.semaphore_signal(barrier, inc=1, device_id=(region, peer), device_id_type=MESH)

    peers(greet)
    for load in loads:
        load.start()
    for load in loads[:3]:
        load.wait()

    lane = iota((atm_blocks, cells), 1)
    level = lane // columns
    level_weight = jnp.zeros((atm_blocks, cells), F32)
    for l in range(cap):
        level_weight = jnp.where(level == l, weights_ref[l], level_weight)
    pieces = []
    for f in range(nf):
        x = atm_ref[:, f * cells : (f + 1) * cells].astype(F32) * level_weight
        x = x + pltpu.roll(x, 2 * columns, 1)
        pieces.append(x + pltpu.roll(x, columns, 1))
    combined = jnp.concatenate(pieces, axis=1)
    block = iota((atm_blocks, nf * cells), 1) % cells // columns
    stacked = jnp.concatenate([jnp.where(block == c, combined, 0.0) for c in range(cap)], axis=0)
    first, second = two_parts(stacked)
    third = (stacked - first.astype(F32) - second.astype(F32)).astype(BF16)
    table = jnp.concatenate([first, second, third], axis=0)
    width = 3 * cap * atm_blocks
    at = iota((width, tiles), 0)
    wanted = jnp.full((width, tiles), -1, jnp.int32)
    for c in range(cap):
        wanted = jnp.where(at // atm_blocks % cap == c, src_ref[0, c : c + 1, :], wanted)
    pick = jnp.where(wanted == at % atm_blocks, 1.0, 0.0).astype(BF16)
    packed = dot(pick, table, ((0,), (0,)))
    early, late = len(EARLY), len(LATE)
    early_words, late_words = early // 2 + 1, late // 2 + 1
    early_rows, late_rows = (0, early_words), (LATE_ROW, late_words)
    largest = jnp.max(jnp.abs(combined), axis=1, keepdims=True)
    largest = jnp.max(largest, axis=0, keepdims=True)
    power = jnp.floor(jnp.log2(jnp.maximum(largest, 1e-30))) + 1.0
    whole = jnp.floor(packed * (STEPS * jnp.exp2(-power)) + 0.5).astype(jnp.int32)
    power = jnp.broadcast_to(power.astype(jnp.int32), (tiles, cells))
    for start, fields in ((0, EARLY), (LATE_ROW, LATE)):
        parts_of = [whole[:, f * cells : (f + 1) * cells] for f in fields] + [power]
        for n in range(len(parts_of) // 2):
            send1[:, start + n, :] = parts_of[2 * n] * 65536 + (parts_of[2 * n + 1] + 32768)

    at = iota((tiles, slots), 1)
    sender = chip_at(at // 8, -1) * 2 + at % 2
    repeat = jnp.where(sender == iota((tiles, slots), 0), 1.0, 0.0)
    by_slot = dot(owner_ref[0].astype(F32).astype(BF16), repeat.astype(BF16))
    own_row = iota((cap, slots), 0) == iota((cap, slots), 1) % 8 // 2
    owner_of = jnp.sum(jnp.where(own_row, by_slot, 0.0), axis=0, keepdims=True)
    feeds = jnp.where(
        owner_of.astype(jnp.int32) == iota((ocean_blocks, slots), 0), 1.0, 0.0
    ).astype(BF16)

    for rows in (early_rows, late_rows):
        recv1[pl.ds(tile, 1), pl.ds(*rows), :] = send1[pl.ds(tile, 1), pl.ds(*rows), :]

    pl.semaphore_wait(barrier, tiles - 1 + (reached if regions > 1 else 0))

    def send(source, target, rows, send_sem, recv_sem, peer):
        pltpu.make_async_remote_copy(
            src_ref=source.at[peer, pl.ds(*rows)],
            dst_ref=target.at[tile, pl.ds(*rows)],
            send_sem=send_sem,
            recv_sem=recv_sem,
            device_id=(region, peer),
            device_id_type=MESH,
        ).start()

    def drain(buffer, count, rows, sem):
        whole = buffer.at[pl.ds(0, count), pl.ds(0, rows)]
        pltpu.make_async_copy(whole, whole, sem).wait()

    peers(lambda n, peer: send(send1, recv1, early_rows, send1_sem, recv1_sem.at[n], peer))
    peers(lambda n, peer: send(send1, recv1, late_rows, late_send_sem, late_recv_sem.at[n], peer))

    for load in loads[3:]:
        load.wait()

    row8 = iota((8, cells), 0)
    lane8 = iota((8, cells), 1)
    own_lanes = row8 // 2 == lane8 // columns
    even = row8 % 2 == 0
    diagonal = [own_lanes & even, own_lanes & (row8 % 2 == 1)]

    def group(g):
        return remap[pl.ds(pl.multiple_of(g * depth, depth), depth), :]

    def forward(k, start, rows_in, column):
        g = chip_at(k, -1)
        halves = []
        for h in range(2):
            values = []
            for n in range(rows_in // 2 + 1):
                word = recv1[g * 2 + h, pl.ds(start + n, 1), :]
                values += [word >> 16, (word & 65535) - 32768]
            scale = jnp.exp2(values[rows_in].astype(F32)) * (1.0 / STEPS)
            rows = [
                jnp.where(
                    diagonal[h],
                    jnp.broadcast_to(value.astype(F32) * scale, (8, cells)),
                    0.0,
                )
                for value in values[:rows_in]
            ]
            halves.append(jnp.concatenate(rows, axis=0))
        high, low = two_parts(jnp.concatenate(halves, axis=1))
        w = group(g)
        out = dot(high, w) + dot(low, w)
        for f in range(rows_in):
            at = (column + f) * cells
            contrib[pl.ds(pl.multiple_of(k * 8, 8), 8), at : at + cells] = out[
                f * 8 : (f + 1) * 8
            ]

    def select(some, columns_in):
        high, low = two_parts(contrib[some, columns_in])
        return dot(feeds[:, some], high) + dot(feeds[:, some], low)

    early_columns, late_columns = slice(0, early * cells), slice(early * cells, nf * cells)
    for n in range(CLASSES):
        drain(recv1, 2 * per_class - (n == CLASSES - 1), early_words, recv1_sem.at[n])

        @pl.loop(n * per_class, (n + 1) * per_class, unroll=min(FORWARD_UNROLL, per_class))
        def _(k):
            forward(k, 0, early, 0)

        part = select(slice(n * per_class * 8, (n + 1) * per_class * 8), early_columns)
        if n == 0:
            total_ref[:, early_columns] = part
        else:
            total_ref[:, early_columns] += part

    place = {f: n for n, f in enumerate(EARLY + LATE)}

    def bottom_of(fields):
        return {f: total_ref[:, place[f] * cells : (place[f] + 1) * cells] for f in fields}

    bottom = bottom_of(EARLY)
    surface = [ocean_ref[:, f * cells : (f + 1) * cells] for f in range(4)]
    transfer, latent, fresh = freshwater_flux(bottom, surface)

    weighted = jnp.sum(area_ref[...] * fresh, axis=0, keepdims=True)
    total = jnp.sum(area_ref[...], axis=0, keepdims=True)
    half = cells // 2
    low_lanes = iota((1, cells), 1) < half
    sums = jnp.where(
        low_lanes, weighted + pltpu.roll(weighted, half, 1), total + pltpu.roll(total, half, 1)
    )
    zrows[pl.ds(region, 1), pl.ds(0, 1), :] = sums.reshape(1, 1, cells)

    def row_copy(source, target, send_sem, recv_sem, device):
        return pltpu.make_async_remote_copy(
            src_ref=source,
            dst_ref=target,
            send_sem=send_sem,
            recv_sem=recv_sem,
            device_id=device,
            device_id_type=MESH,
        )

    for r in range(roots):

        @pl.when(region != r)
        def _():
            row = zrows.at[region, pl.ds(0, 1)]
            row_copy(row, row, zsend_sem.at[r], zrecv_sem, (r, tile)).start()

    for n in range(CLASSES):
        drain(recv1, 2 * per_class - (n == CLASSES - 1), late_words, late_recv_sem.at[n])

        @pl.loop(n * per_class, (n + 1) * per_class, unroll=min(FORWARD_UNROLL, per_class))
        def _(k):
            forward(k, LATE_ROW, late, early)

    total_ref[:, late_columns] = select(slice(0, slots), late_columns)
    bottom.update(bottom_of(LATE))
    raw = fluxes(bottom, surface, transfer, latent, fresh)
    for f in range(nflx):
        if f != 6:
            ocean_out[:, f * cells : (f + 1) * cells] = raw[f]
    out_parts = [slice(0, 6 * cells), slice(7 * cells, nflx * cells), slice(6 * cells, 7 * cells)]
    stores = [
        pltpu.make_async_copy(ocean_out.at[:, p], ocean_hbm_out.at[:, p], out_sem.at[n])
        for n, p in enumerate(out_parts)
    ] + [pltpu.make_async_copy(atm_out, atm_hbm_out, out_sem.at[3])]
    stores[0].start()
    stores[1].start()
    fresh_high, fresh_low = two_parts(fresh)
    fields = [r.astype(BF16) for r in raw]
    fields[6] = fresh_high
    rows_back[...] = dot(feeds, jnp.concatenate(fields + [fresh_low], axis=1), ((0,), (0,)))
    ones = jnp.ones((8, cells), F32)

    def pair(a, b):
        upper = row8 < 4
        return jnp.where(upper, a, b) + pltpu.roll(jnp.where(upper, b, a), 4, 0)

    def four(a, b):
        near = row8 % 4 < 2
        x = jnp.where(near, b, a)
        return jnp.where(near, a, b) + jnp.where(near, pltpu.roll(x, 6, 0), pltpu.roll(x, 2, 0))

    def backward(k):
        g = chip_at(k, -1)
        at_rows = pl.ds(pl.multiple_of(k * 8, 8), 8)
        rows = [rows_back[at_rows, f * cells : (f + 1) * cells] for f in range(nflx + 1)]
        left = jnp.concatenate(rows + [ones], axis=0).astype(BF16)
        out = dot(left, group(g), ((1,), (1,)))
        x = []
        for f in range(nflx + 1):
            piece = out[f * 8 : (f + 1) * 8]
            mixed = jnp.where(even, piece[:, :cells], piece[:, cells:])
            x.append(jnp.where(own_lanes, mixed, 0.0))
        x[6] = x[6] + x[nflx]
        q0 = four(pair(x[0], x[4]), pair(x[2], x[6]))
        q1 = four(pair(x[1], x[5]), pair(x[3], x[7]))
        send2[g * 2, pl.ds(0, 8), :] = jnp.where(even, q0, pltpu.roll(q1, 1, 0))
        send2[g * 2 + 1, pl.ds(0, 8), :] = jnp.where(even, pltpu.roll(q0, 7, 0), q1)
        for h in range(2):
            at = (nflx + 1) * 8
            send2[g * 2 + h, pl.ds(nflx, 1), :] = out[at : at + 1, h * cells : (h + 1) * cells]

    def send_back(k):
        chip = chip_at(k, -1)
        for peer in (chip * 2 + core, chip * 2 + 1 - core):
            send(send2, recv2, (0, nflx + 1), send2_sem, recv2_sem, peer)

    whole_steps = (chips - 1) // BACK_STEP

    @pl.loop(0, whole_steps)
    def _(i):
        for u in range(BACK_STEP):
            backward(i * BACK_STEP + u)
        for u in range(BACK_STEP):
            send_back(i * BACK_STEP + u)

    for k in range(whole_steps * BACK_STEP, chips):
        backward(k)
    for k in range(whole_steps * BACK_STEP, chips - 1):
        send_back(k)
    send(send2, recv2, (0, nflx + 1), send2_sem, recv2_sem, my_chip * 2 + 1 - core)
    recv2[pl.ds(tile, 1), pl.ds(0, nflx + 1), :] = send2[pl.ds(tile, 1), pl.ds(0, nflx + 1), :]

    @pl.when(is_root)
    def _():
        if regions > 1:
            drain(zrows, regions - 1, 1, zrecv_sem)
        column = jnp.sum(zrows[:, 0, :], axis=0, keepdims=True)
        trows[pl.ds(tile, 1), pl.ds(0, 1), :] = column.reshape(1, 1, cells)

        def send_sums(_, peer):
            row = trows.at[tile, pl.ds(0, 1)]
            row_copy(row, row, tsend_sem, trecv_sem, (region, peer)).start()

        peers(send_sums)

    drain(recv2, tiles - 1, nflx + 1, recv2_sem)
    lane_group = iota((atm_blocks, cells), 1) // columns

    def gather(rows):
        found = dot(pick[: cap * atm_blocks], jnp.concatenate(rows, axis=1).astype(BF16))
        outs = []
        for n in range(len(rows)):
            x = jnp.zeros((atm_blocks, cells), F32)
            for c in range(cap):
                x = jnp.where(
                    lane_group == c,
                    found[c * atm_blocks : (c + 1) * atm_blocks, n * cells : (n + 1) * cells],
                    x,
                )
            x = x + pltpu.roll(x, 2 * columns, 1)
            outs.append(x + pltpu.roll(x, columns, 1))
        return outs

    outs = gather([recv2[:, f, :] for f in range(nflx) if f != 6])
    exact = [x.astype(F32) for f in (6, nflx) for x in two_parts(recv2[:, f, :])]
    fresh_high, fresh_low, ones_high, ones_low = gather(exact)
    fresh_back, ones_back = fresh_high + fresh_low, ones_high + ones_low

    @pl.when(is_root)
    def _():
        drain(trows, tiles - 1, 1, trecv_sem)
        everything = jnp.sum(trows[:, 0, :], axis=0, keepdims=True)
        zmean[1, pl.ds(0, 1), :] = everything

    if regions > roots:

        @pl.when(jnp.logical_not(is_root))
        def _():
            drain(zmean, 1, 1, mrecv_sem)

        def send_mean(peer):
            mean = zmean.at[1, pl.ds(0, 1)]
            row_copy(mean, mean, msend_sem, mrecv_sem, (peer, tile)).start()

        @pl.when(region == teller)
        def _():
            @pl.loop(roots, near)
            def _(r):
                send_mean(r)

        @pl.when(hands_on)
        def _():
            send_mean(region + stride)

    sums_all = zmean[1, pl.ds(0, 1), :]
    weighted_all = jnp.sum(jnp.where(low_lanes, sums_all, 0.0), axis=1, keepdims=True)
    area_all = jnp.sum(jnp.where(low_lanes, 0.0, sums_all), axis=1, keepdims=True)
    shift = weighted_all / area_all
    ocean_out[:, 6 * cells : 7 * cells] = fresh - shift
    stores[2].start()
    outs.insert(6, fresh_back - shift * ones_back)
    for t in range(nflx // cap):
        x = outs[t * cap]
        for c in range(1, cap):
            x = jnp.where(lane_group == c, outs[t * cap + c], x)
        atm_out[:, t * cells : (t + 1) * cells] = x
    stores[3].start()

    drain(send1, tiles - 1, early_words, send1_sem)
    drain(send1, tiles - 1, late_words, late_send_sem)
    drain(send2, tiles - 1, nflx + 1, send2_sem)
    for r in range(roots):

        @pl.when(region != r)
        def _():
            drain(zrows, 1, 1, zsend_sem.at[r])

    @pl.when(is_root)
    def _():
        drain(trows, tiles - 1, 1, tsend_sem)

    if regions > roots:
        if near > roots:

            @pl.when(region == teller)
            def _():
                drain(zrows, near - roots, 1, msend_sem)

        @pl.when(hands_on)
        def _():
            drain(zrows, 1, 1, msend_sem)

    for store in stores:
        store.wait()


def copy_out(ocean_in, atm_in, ocean_out, atm_out, ocean_held, atm_held, sem):
    height = ocean_in.shape[0] // PIECES
    legs = [(atm_in, atm_held, atm_out)]
    for n in range(PIECES):
        rows = pl.ds(n * height, height)
        legs.append((ocean_in.at[rows], ocean_held.at[rows], ocean_out.at[rows]))
    arrivals = [
        pltpu.make_async_copy(source, held, sem.at[0, n])
        for n, (source, held, _) in enumerate(legs)
    ]
    leaves = [
        pltpu.make_async_copy(held, target, sem.at[1, n])
        for n, (_, held, target) in enumerate(legs)
    ]
    for arrival in arrivals:
        arrival.start()
    for arrival, leave in zip(arrivals, leaves):
        arrival.wait()
        leave.start()
    for leave in leaves:
        leave.wait()


def per_device(
    regions, tiles, atm_state, ocean_state, cell_area, level_weights, remap, send_src, recv_ocn
):
    cap = send_src.shape[2]
    slots = tiles * cap
    atm_blocks = atm_state.shape[0]
    ocean_blocks, cells = cell_area.shape
    columns = remap.shape[1]
    nf = atm_state.shape[1] // cells
    nflx = 8
    hbm = pl.BlockSpec(memory_space=pl.ANY)
    box = pltpu.VMEM((tiles, 16, cells), F32)
    dma = pltpu.SemaphoreType.DMA
    results = (
        jax.ShapeDtypeStruct((ocean_blocks, nflx * cells), F32),
        jax.ShapeDtypeStruct((atm_blocks, nflx * columns), F32),
    )
    made = pl.pallas_call(
        functools.partial(kernel, regions, tiles),
        out_shape=results,
        in_specs=[hbm, hbm, hbm, pl.BlockSpec(memory_space=pltpu.SMEM), hbm, hbm, hbm],
        out_specs=(hbm, hbm),
        scratch_shapes=[
            pltpu.VMEM(atm_state.shape, BF16),
            pltpu.VMEM(ocean_state.shape, F32),
            pltpu.VMEM(cell_area.shape, F32),
            pltpu.VMEM((1, cap, tiles), jnp.int32),
            pltpu.VMEM((1, cap, tiles), jnp.int32),
            pltpu.VMEM(results[0].shape, F32),
            pltpu.VMEM(results[1].shape, F32),
            pltpu.VMEM((slots * columns, cells), BF16),
            pltpu.VMEM((tiles, 8, cells), jnp.int32),
            pltpu.VMEM((tiles, 8, cells), jnp.int32),
            pltpu.VMEM((slots, nf * cells), F32),
            pltpu.VMEM((ocean_blocks, nf * cells), F32),
            pltpu.VMEM((slots, (nflx + 1) * cells), F32),
            box,
            box,
            pltpu.VMEM((tiles, 8, cells), F32),
            pltpu.VMEM((regions, 8, cells), F32),
            pltpu.VMEM((2, 8, cells), F32),
            pltpu.SemaphoreType.DMA((6,)),
            dma,
            pltpu.SemaphoreType.DMA((CLASSES,)),
            dma, dma, dma, dma,
            pltpu.SemaphoreType.DMA((ROOTS,)),
            dma, dma, dma, dma,
            pltpu.SemaphoreType.DMA((CLASSES,)),
            pltpu.SemaphoreType.DMA((4,)),
        ],
        compiler_params=pltpu.CompilerParams(
            collective_id=0, has_side_effects=True, vmem_limit_bytes=60 * 1024 * 1024
        ),
        cost_estimate=pl.CostEstimate(
            flops=400_000_000, bytes_accessed=4_000_000, transcendentals=100_000
        ),
        name="couple",
    )(
        atm_state, ocean_state, cell_area, level_weights,
        remap.reshape(slots * columns, cells),
        jnp.swapaxes(send_src, 1, 2), jnp.swapaxes(recv_ocn, 1, 2),
    )
    return pl.pallas_call(
        copy_out,
        out_shape=results,
        in_specs=[hbm, hbm],
        out_specs=(hbm, hbm),
        scratch_shapes=[
            pltpu.VMEM(results[0].shape, F32),
            pltpu.VMEM(results[1].shape, F32),
            pltpu.SemaphoreType.DMA((2, PIECES + 1)),
        ],
        compiler_params=pltpu.CompilerParams(vmem_limit_bytes=60 * 1024 * 1024),
        name="results",
    )(*made)


def solution(mesh):
    in_specs = (
        P(("region", "tile"), None),
        P(("region", "tile"), None),
        P(("region", "tile"), None),
        P(),
        P(("region", "tile"), None, None),
        P(("region", "tile"), None, None),
        P(("region", "tile"), None, None),
    )
    out_specs = (P(("region", "tile"), None), P(("region", "tile"), None))
    return jax.shard_map(
        functools.partial(per_device, mesh.shape["region"], mesh.shape["tile"]),
        mesh=mesh,
        in_specs=in_specs,
        out_specs=out_specs,
        check_vma=False,
    )
```
